128 devices in a mesh: dp: 16 (over y, x), serve: 8 (over z, core).
Axes of the slice: x: 4, y: 4, z: 4, core: 2. Of those that a mesh axis runs over, the one named last changes fastest.
Arguments:
- inputs: bfloat16 [16384, 8192], P('dp', 'serve'), may hold values from -6 to 6
- cotangent: bfloat16 [16384, 4608], P('dp'), may hold values from -0.046875 to 0.046875
- master: float32 [8, 576, 128, 128], P('serve', 'dp'), may hold values from -0.12 to 0.12
- moment: float32 [8, 576, 128, 128], P('serve', 'dp'), may hold values from -1.8 to 1.8
- variance: float32 [8, 576, 128, 128], P('serve', 'dp'), may hold values from 0.01 to 1
- slice_start: int32 [16], replicated, may hold values from 0 to 279, as said below
- block_owner: int32 [36], replicated, may hold values from 0 to 7, as said below
- group_heads: int32 [32], replicated, may hold values from 0 to 31, each once
Outputs:
- new_master: float32 [8, 576, 128, 128], P('serve', 'dp')
- new_moment: float32 [8, 576, 128, 128], P('serve', 'dp')
- new_variance: float32 [8, 576, 128, 128], P('serve', 'dp')
- served_blocks: bfloat16 [8, 9, 8192, 128], P('serve', None, 'dp')
- served_scales: bfloat16 [8, 9, 64], P('serve', None, 'dp')
The draws below stay inside these ranges and needn't reach their ends.
Inputs may be any that keep to these rules, and one draw needn't show every extreme that they name: Starts never fall; slice_start[0] = 0; every slice_start[i] lies within 9 blocks of i * 18, so a slice holds at most 36 blocks, and some rank's slice holds exactly 36. `block_owner`: each serving rank owns at most 9 packed column blocks, and some rank owns exactly 9.
All inputs are finite; a program needn't handle non-finite values.
Results may differ from the reference program's by a relative error of at most 0.024.
Values may be sent and summed in bfloat16 or wider, within the bound.
No kernel may reach another device: no remote copies, remote signals or barrier semaphores. Data moves between devices by JAX's collectives and lax.ppermute only.
A program may use at most 128 MiB of HBM per device.

```python
import math
import jax
import jax.numpy as jnp
from jax import lax

ROWS = 8192
QPER = 16
GROUPS = 2
BLK = 128
TOK_DEV = 1024
QHEADS = 32
CBG = 18
CB = 36
COLS = 4608
RB = 64
RBS = 8
NBS = 288
SLICE = 18
CAP = 36
SCAP = 9
TOKENS = 16384
N_DP = 16
N_SERVE = 8


def draw_slice_start(key, part):
    key = jax.random.fold_in(key, 11)
    key_shift, key_star = jax.random.split(key)
    half_slice = SLICE // 2
    rank_ids = jnp.arange(N_DP, dtype=jnp.int32)
    shifts = jax.random.randint(key_shift, (N_DP,), -half_slice, half_slice + 1, dtype=jnp.int32)
    widest = jax.random.randint(key_star, (), 1, N_DP - 1, dtype=jnp.int32)
    shifts = jnp.where(rank_ids == widest, -half_slice, shifts)
    shifts = jnp.where(rank_ids == widest + 1, half_slice, shifts)
    shifts = jnp.where(rank_ids == N_DP - 1, half_slice, shifts)
    shifts = jnp.where(rank_ids == 0, 0, shifts)
    return rank_ids * SLICE + shifts


def draw_block_owner(key, part):
    key = jax.random.fold_in(key, 23)
    key_order, key_star = jax.random.split(key)
    order = jax.random.permutation(key_order, CB).astype(jnp.int32)
    busiest = jax.random.randint(key_star, (), 0, N_SERVE, dtype=jnp.int32)
    places = jnp.arange(CB, dtype=jnp.int32)
    others = (busiest + 1 + (places - SCAP) % (N_SERVE - 1)) % N_SERVE
    ranks = jnp.where(places < SCAP, busiest, others).astype(jnp.int32)
    return jnp.zeros((CB,), jnp.int32).at[order].set(ranks)


def block_levels(stream_key, shape, cuts, least, high):
    gain = 1.0
    for position, shards_of in cuts:
        draws = jax.random.uniform(jax.random.fold_in(jax.random.fold_in(stream_key, 6), position), (shards_of,), jnp.float32, least / len(cuts), high / len(cuts))
        gain = gain * jnp.repeat(jnp.exp(draws), shape[position] // shards_of).reshape((-1,) + (1,) * (len(shape) - 1 - position))
    return gain


def bell_draw(key, shape, spread, bound, cuts=(), kind=jnp.bfloat16):
    result = jax.random.normal(key, shape, jnp.float32) * spread
    if len(cuts) > 0:
        result = block_levels(key, shape, cuts, -0.22, 0.18) * result
    return jnp.clip(result, min=-bound, max=bound).astype(kind)


def setup_inputs(seed: int = 0) -> dict:
    streams_of = jax.random.split(jax.random.key(seed), 9)
    return {
        "inputs": bell_draw(streams_of[0], (TOKENS, ROWS), 1.0, 6.0, ((0, 16), (1, 8))),
        "cotangent": bell_draw(streams_of[1], (TOKENS, COLS), (TOK_DEV * N_DP) ** -0.5, 0.046875, ((0, 16),)),
        "master": bell_draw(streams_of[2], (N_SERVE, N_DP * CAP, BLK, BLK), 0.02, 0.12, ((0, 8), (1, 16)), jnp.float32),
        "moment": bell_draw(streams_of[3], (N_SERVE, N_DP * CAP, BLK, BLK), 0.3, 1.8, ((0, 8), (1, 16)), jnp.float32),
        "variance": jnp.clip(jnp.exp(math.log(1.0) - 4.6051702 * jax.random.uniform(streams_of[4], (N_SERVE, N_DP * CAP, BLK, BLK), jnp.float32) ** block_levels(streams_of[4], (N_SERVE, N_DP * CAP, BLK, BLK), ((0, 8), (1, 16)), -0.2, 0.2)), 0.01, 1.0),
        "slice_start": draw_slice_start(jax.random.fold_in(streams_of[8], 71), 0),
        "block_owner": draw_block_owner(jax.random.fold_in(streams_of[8], 71), 0),
        "group_heads": jax.random.permutation(streams_of[7], QHEADS).astype(jnp.int32),
    }


first_bias = 1.0 - 0.9 ** 10
second_bias = 1.0 - 0.95 ** 10

def reference(inputs, cotangent, master, moment, variance, slice_start, block_owner, group_heads):

    def accumulate(rank_id, running_sum):
        tok_inputs = lax.dynamic_slice_in_dim(inputs, rank_id * TOK_DEV, TOK_DEV, 0)
        tok_grads = lax.dynamic_slice_in_dim(cotangent, rank_id * TOK_DEV, TOK_DEV, 0)
        gradient = jnp.dot(tok_inputs.T, tok_grads, preferred_element_type=jnp.float32).astype(jnp.bfloat16)
        return running_sum + gradient.astype(jnp.float32)
    summed = lax.fori_loop(0, N_DP, accumulate, jnp.zeros((ROWS, COLS), jnp.float32))
    blocks_view = summed.reshape(N_SERVE, RBS, BLK, CB, BLK)
    slot_ids = jnp.arange(N_DP * CAP, dtype=jnp.int32)
    rank_ids = slot_ids // CAP
    offsets = slot_ids % CAP
    slice_ends = jnp.concatenate([slice_start[1:], jnp.full((1,), NBS, jnp.int32)])
    counts = slice_ends - slice_start
    flat_ids = jnp.minimum(slice_start[rank_ids] + offsets, NBS - 1)
    live_mask = offsets < counts[rank_ids]
    shard_ids = jnp.arange(N_SERVE, dtype=jnp.int32)
    slot_grad = blocks_view[shard_ids[:, None], (flat_ids // CB)[None, :], :, (flat_ids % CB)[None, :], :]
    slot_grad = jnp.where(live_mask[None, :, None, None], slot_grad, jnp.float32(0.0))
    new_moment = 0.9 * moment + 0.1 * slot_grad
    new_variance = 0.95 * variance + 0.05 * slot_grad * slot_grad
    new_master = master - 0.02 * (new_moment / first_bias / (jnp.sqrt(new_variance / second_bias) + 1e-08) + 0.1 * master)
    peak_abs = lax.optimization_barrier(jnp.max(jnp.abs(new_master), axis=(2, 3)))
    slot_scale = (peak_abs + 1e-06).astype(jnp.bfloat16)
    slot_code = (new_master / slot_scale.astype(jnp.float32)[:, :, None, None]).astype(jnp.bfloat16)
    packed = jnp.arange(CB, dtype=jnp.int32)
    groups_of = packed // CBG
    within = packed % CBG
    head_ids = group_heads[groups_of * QPER + jnp.minimum(within, QPER - 1)]
    train_col = jnp.where(within < QPER, head_ids, jnp.where(within == QPER, QHEADS + groups_of, QHEADS + GROUPS + groups_of))
    earlier = (block_owner[None, :] == block_owner[:, None]) & (packed[None, :] < packed[:, None])
    slot_of = lax.optimization_barrier(jnp.sum(earlier.astype(jnp.int32), axis=1)).astype(jnp.int32)
    row_global = jnp.arange(RB, dtype=jnp.int32)
    shard_of_row = row_global // RBS
    flat_of = (row_global % RBS)[None, :] * CB + train_col[:, None]
    rank_of = (lax.optimization_barrier(jnp.sum((slice_start[None, None, :] <= flat_of[:, :, None]).astype(jnp.int32), axis=-1)) - 1).astype(jnp.int32)
    slot_index = rank_of * CAP + flat_of - slice_start[rank_of]
    chosen = slot_code[shard_of_row[None, :], slot_index]
    chosen_scale = slot_scale[shard_of_row[None, :], slot_index]
    served = jnp.zeros((N_SERVE, SCAP, RB, BLK, BLK), jnp.bfloat16).at[block_owner, slot_of].set(chosen)
    served_blocks = served.reshape(N_SERVE, SCAP, ROWS, BLK)
    served_scales = jnp.zeros((N_SERVE, SCAP, RB), jnp.bfloat16).at[block_owner, slot_of].set(chosen_scale)
    return (new_master, new_moment, new_variance, served_blocks, served_scales)
```

```python
import jax
import jax.numpy as jnp
from jax import lax
from jax.experimental import pallas as pl
from jax.experimental.pallas import tpu as pltpu
from jax.sharding import PartitionSpec as P

QPER = 16
GROUPS = 2
BLK = 128
HALF = 64
UNIT = 9
WIDE = UNIT * BLK
CAP = 36
COLS = 36
SCAP = 9
MSG = SCAP * HALF + 16

first_bias = 1.0 - 0.9**10
second_bias = 1.0 - 0.95**10

BF = jnp.bfloat16
F32 = jnp.float32


def cost(flops, nbytes):
    return pl.CostEstimate(flops=flops, bytes_accessed=nbytes, transcendentals=0)


def params(mib=48):
    return pltpu.CompilerParams(vmem_limit_bytes=mib * 1024 * 1024)


def mm_body(table, left_a, left_b, right, out):
    left = jnp.concatenate([left_a[...], left_b[...]], axis=1)
    prod = lax.dot_general(
        left, right[...], (((0,), (0,)), ((), ())), preferred_element_type=F32
    )
    out[0] = prod[:BLK].astype(BF)
    out[1] = prod[BLK:].astype(BF)


def mm(table, inputs, cotangent):
    n = table.shape[1]
    tok = inputs.shape[0]
    return pl.pallas_call(
        mm_body,
        grid_spec=pltpu.PrefetchScalarGridSpec(
            num_scalar_prefetch=1,
            grid=(n,),
            in_specs=[
                pl.BlockSpec((tok, BLK), lambda g, t: (0, t[0, g])),
                pl.BlockSpec((tok, BLK), lambda g, t: (0, t[1, g])),
                pl.BlockSpec((tok, WIDE), lambda g, t: (0, t[2, g])),
            ],
            out_specs=pl.BlockSpec((2, BLK, WIDE), lambda g, t: (g, 0, 0)),
        ),
        out_shape=jax.ShapeDtypeStruct((2 * n, BLK, WIDE), BF),
        compiler_params=params(),
        cost_estimate=cost(
            2 * n * 256 * WIDE * tok, n * tok * (WIDE + 256) * 2 + n * 256 * WIDE * 2
        ),
        name="gradient_pieces",
    )(table, inputs, inputs, cotangent)


def adam_body(
    info, halo_b, grad_a, grad_b, halo_a, master, moment, variance,
    new_master, new_moment, new_variance, send3, send1, keep1, keep3,
    window, mine, other, scales,
):
    step = pl.program_id(0)
    off, length, odd = info[0], info[1], info[2]

    @pl.when(step == 0)
    def _():
        window[0] = halo_b[...]
        window[1] = grad_a[...]
        window[2] = grad_b[...]
        window[3] = halo_a[...]

    for n in range(4):
        slot = step * 4 + n
        place = off + slot
        place = jnp.where(place >= CAP, place - CAP, place)
        unit = lax.div(place, UNIT)
        lanes = pl.ds(pl.multiple_of((place - unit * UNIT) * BLK, BLK), BLK)
        live = slot < length
        grad = jnp.where(live, window[unit, :, lanes].astype(F32), 0.0)
        mom = 0.9 * moment[0, n] + 0.1 * grad
        var = 0.95 * variance[0, n] + 0.05 * (grad * grad)
        old = master[0, n]
        new = old - 0.02 * (
            (mom * (1.0 / first_bias)) / (jnp.sqrt(var * (1.0 / second_bias)) + 1e-08) + 0.1 * old
        )
        new_master[0, n] = new
        new_moment[0, n] = mom
        new_variance[0, n] = var
        peak = jnp.max(jnp.abs(new), axis=(0, 1), keepdims=True)
        scale = (peak + 1e-06).astype(BF).astype(F32)
        code = jnp.where(live, new * (1.0 / scale), 0.0).astype(BF)
        spot = jnp.where(odd == 1, unit, lax.rem(unit + 3, 4))
        top, low = code[:HALF], code[HALF:]
        mine[spot, :, lanes] = jnp.where(odd == 1, low, top)
        other[spot, :, lanes] = jnp.where(odd == 1, top, low)
        scales[spot, :, lanes] = jnp.broadcast_to(jnp.where(live, scale, 0.0), (8, BLK))

    @pl.when(step == pl.num_programs(0) - 1)
    def _():
        tail = jnp.concatenate(
            [scales[q, 0:1] for q in range(4)] + [jnp.zeros((12, WIDE), F32)], axis=0
        ).astype(BF)
        for q in range(3):
            send3[q * HALF : (q + 1) * HALF] = other[q]
            keep3[q * HALF : (q + 1) * HALF] = mine[q]
        send3[3 * HALF :] = tail
        keep3[3 * HALF :] = tail
        send1[:HALF] = other[3]
        send1[HALF:] = tail
        keep1[:HALF] = mine[3]
        keep1[HALF:] = tail


def adam(info, halo_b, grad_a, grad_b, halo_a, master, moment, variance):
    whole = lambda rows: pl.BlockSpec((rows, WIDE), lambda s, t: (0, 0))
    state = pl.BlockSpec((1, 4, BLK, BLK), lambda s, t: (0, s, 0, 0))
    wide = lambda rows: jax.ShapeDtypeStruct((rows, WIDE), BF)
    slots = jax.ShapeDtypeStruct(master.shape, F32)
    return pl.pallas_call(
        adam_body,
        grid_spec=pltpu.PrefetchScalarGridSpec(
            num_scalar_prefetch=1,
            grid=(CAP // 4,),
            in_specs=[whole(BLK)] * 4 + [state] * 3,
            out_specs=[state] * 3
            + [whole(3 * HALF + 16), whole(HALF + 16), whole(HALF + 16), whole(3 * HALF + 16)],
            scratch_shapes=[
                pltpu.VMEM((4, BLK, WIDE), BF),
                pltpu.VMEM((4, HALF, WIDE), BF),
                pltpu.VMEM((4, HALF, WIDE), BF),
                pltpu.VMEM((4, 8, WIDE), F32),
            ],
        ),
        out_shape=[slots] * 3
        + [wide(3 * HALF + 16), wide(HALF + 16), wide(HALF + 16), wide(3 * HALF + 16)],
        compiler_params=params(),
        cost_estimate=cost(36 * 16384 * 20, 36 * 16384 * 28),
        name="adam_slots",
    )(info, halo_b, grad_a, grad_b, halo_a, master, moment, variance)


def pack_body(info, keep3, got3, got1, got2, out, row, tails):
    odd = info[0]

    def take(ref, q):
        return ref[q * HALF : (q + 1) * HALF]

    def tail(ref, n):
        return ref[n * HALF :].astype(F32)

    @pl.when(odd == 0)
    def _():
        row[0] = take(keep3, 0) + got1[:HALF]
        row[1] = take(keep3, 1) + take(got3, 0)
        row[2] = take(keep3, 2) + take(got3, 1)
        row[3] = take(got3, 2) + got2[:HALF]
        own, pair, near, far = tail(keep3, 3), tail(got3, 3), tail(got1, 1), tail(got2, 1)
        tails[0, 0:1] = own[0:1] + near[3:4]
        tails[1, 0:1] = own[1:2] + pair[0:1]
        tails[2, 0:1] = own[2:3] + pair[1:2]
        tails[3, 0:1] = pair[2:3] + far[3:4]

    @pl.when(odd == 1)
    def _():
        row[0] = take(got3, 0) + got2[:HALF]
        row[1] = take(keep3, 0) + take(got3, 1)
        row[2] = take(keep3, 1) + take(got3, 2)
        row[3] = take(keep3, 2) + got1[:HALF]
        own, pair, near, far = tail(keep3, 3), tail(got3, 3), tail(got1, 1), tail(got2, 1)
        tails[0, 0:1] = pair[0:1] + far[3:4]
        tails[1, 0:1] = own[0:1] + pair[1:2]
        tails[2, 0:1] = own[1:2] + pair[2:3]
        tails[3, 0:1] = own[2:3] + near[3:4]

    def owner(o, carry):
        rows = []
        for t in range(SCAP):
            col = info[1 + o * SCAP + t]
            held = jnp.maximum(col, 0)
            unit = lax.div(held, UNIT)
            lanes = pl.ds(pl.multiple_of((held - unit * UNIT) * BLK, BLK), BLK)
            piece = row[unit, :, lanes]
            out[o, t * HALF : (t + 1) * HALF] = jnp.where(col >= 0, piece, jnp.zeros_like(piece))
            rows.append(jnp.where(col >= 0, tails[unit, :, lanes][0:1], 0.0))
        rows.append(jnp.zeros((16 - SCAP, BLK), F32))
        out[o, SCAP * HALF :] = jnp.concatenate(rows, axis=0).astype(BF)
        return carry

    lax.fori_loop(0, 8, owner, 0)


def pack(info, keep3, got3, got1, got2):
    return pl.pallas_call(
        pack_body,
        grid_spec=pltpu.PrefetchScalarGridSpec(
            num_scalar_prefetch=1,
            grid=(1,),
            in_specs=[
                pl.BlockSpec(a.shape, lambda s, t: (0, 0)) for a in (keep3, got3, got1, got2)
            ],
            out_specs=pl.BlockSpec((8, MSG, BLK), lambda s, t: (0, 0, 0)),
            scratch_shapes=[pltpu.VMEM((4, HALF, WIDE), BF), pltpu.VMEM((4, 8, WIDE), F32)],
        ),
        out_shape=jax.ShapeDtypeStruct((8, MSG, BLK), BF),
        compiler_params=params(),
        cost_estimate=cost(0, 3 * 8 * MSG * BLK * 2),
        name="pack_by_owner",
    )(info, keep3, got3, got1, got2)


def split_body(info, got, *outs):
    for j, out in enumerate(outs):
        out[...] = got[info[j]]


def split(info, got):
    return pl.pallas_call(
        split_body,
        grid_spec=pltpu.PrefetchScalarGridSpec(
            num_scalar_prefetch=1,
            grid=(1,),
            in_specs=[pl.BlockSpec(got.shape, lambda s, t: (0, 0, 0))],
            out_specs=[pl.BlockSpec(got.shape[1:], lambda s, t: (0, 0))] * 8,
        ),
        out_shape=[jax.ShapeDtypeStruct(got.shape[1:], BF)] * 8,
        compiler_params=params(),
        cost_estimate=cost(0, 2 * 8 * MSG * BLK * 2),
        name="split_by_band",
    )(info, got)


def place_body(info, *refs):
    out, tails = refs[8], refs[9]
    for j in range(8):
        at = info[j]
        for t in range(SCAP):
            out[0, t, pl.ds(pl.multiple_of(at * HALF, HALF), HALF)] = refs[j][
                t * HALF : (t + 1) * HALF
            ]
        tails[at] = refs[j][SCAP * HALF :]


def place(info, pieces):
    return pl.pallas_call(
        place_body,
        grid_spec=pltpu.PrefetchScalarGridSpec(
            num_scalar_prefetch=1,
            grid=(1,),
            in_specs=[pl.BlockSpec((MSG, BLK), lambda s, t: (0, 0))] * 8,
            out_specs=[
                pl.BlockSpec((1, SCAP, 8 * HALF, BLK), lambda s, t: (0, 0, 0, 0)),
                pl.BlockSpec((8, 16, BLK), lambda s, t: (0, 0, 0)),
            ],
        ),
        out_shape=[
            jax.ShapeDtypeStruct((1, SCAP, 8 * HALF, BLK), BF),
            jax.ShapeDtypeStruct((8, 16, BLK), BF),
        ],
        compiler_params=params(),
        cost_estimate=cost(0, 2 * 8 * MSG * BLK * 2),
        name="place_served",
    )(info, *pieces)


def add(*parts):
    total = parts[0].astype(F32)
    for part in parts[1:]:
        total = total + part.astype(F32)
    return total.astype(BF)


def shards(inputs, cotangent, master, moment, variance, slice_start, block_owner, group_heads):
    me = lax.axis_index("dp").astype(jnp.int32)
    shard = lax.axis_index("serve").astype(jnp.int32)
    y, x = me // 4, me % 4
    ranks = range(16)

    def along_x(k):
        return [(i, i // 4 * 4 + (i + k) % 4) for i in ranks]

    def along_y(k):
        return [(i, (i + 4 * k) % 16) for i in ranks]

    def send(v, pairs):
        return lax.ppermute(v, "dp", pairs)

    def first(k, half):
        to_x = (x + k) % 4
        rows = [2 * ((y + j) % 4) + to_x // 2 for j in ((0, 2) if half == 0 else (1, 3))]
        return rows[0], rows[1], (to_x % 2) * 2

    def last(k, half):
        to_y = (y + k) % 4
        tos = [(x + j) % 4 for j in ((0, 2) if half == 0 else (1, 3))]
        return 2 * to_y + tos[0] // 2, 2 * to_y + tos[1] // 2, (tos[0] % 2) * 2 + 1

    def pieces(groups):
        table = jnp.stack([jnp.stack([g[n] for g in groups]) for n in range(3)])
        return mm(table.astype(jnp.int32), inputs, cotangent)

    def long_send(which, along):
        fwd = pieces([which(2, 0), which(1, 1)])
        got_fwd = send(fwd, along(1))
        bwd = pieces([which(2, 1), which(3, 0)])
        got_bwd = send(bwd, along(-1))
        return got_fwd, got_bwd

    a_fwd, a_bwd = long_send(first, along_x)
    b_fwd, b_bwd = long_send(last, along_y)
    rest_a = pieces([first(1, 0), first(3, 1), first(0, 0), first(0, 1)])
    rest_b = pieces([last(1, 0), last(3, 1), last(0, 0), last(0, 1)])

    def long_end(rest, fwd, bwd, along):
        fwd2 = send(add(rest[0:2], fwd[0:2]), along(1))
        bwd2 = send(add(rest[2:4], bwd[0:2]), along(-1))
        even = add(rest[4:6], fwd2, bwd[2:4])
        odd = add(rest[6:8], bwd2, fwd[2:4])
        return even[0], odd[0], even[1], odd[1]

    part_a = long_end(rest_a, a_fwd, a_bwd, along_x)
    part_b = long_end(rest_b, b_fwd, b_bwd, along_y)

    def short(parts, along):
        got = [send(parts[k], along(k)) for k in (2, 1, 3)]
        return add(parts[0], *got)

    grad_a = short(part_a, along_y)
    grad_b = short(part_b, along_x)
    halo_a = send(grad_a, [(i + 1, i) for i in range(15)])
    halo_b = send(grad_b, [(i, i + 1) for i in range(15)])

    flat = 16 * 18
    ends = jnp.concatenate([slice_start[1:], jnp.full((1,), flat, jnp.int32)])
    is_me = jnp.arange(16, dtype=jnp.int32) == me
    start = jnp.sum(jnp.where(is_me, slice_start, 0))
    end = jnp.sum(jnp.where(is_me, ends, 0))
    odd = x % 2
    info = jnp.stack([start - (18 * me - 9), end - start, odd]).astype(jnp.int32)
    new_master, new_moment, new_variance, send3, send1, keep1, keep3 = adam(
        info, halo_b, grad_a, grad_b, halo_a, master, moment, variance
    )

    got3 = send(send3, [(i, i ^ 1) for i in ranks])
    got1 = send(
        send1, [(i, i - 1 if i % 2 == 0 else i + 1) for i in ranks if 0 < i < 15]
    )
    got2 = send(
        keep1,
        [
            (i, i - 2 if i % 2 == 0 else i + 2)
            for i in ranks
            if 0 <= (i - 2 if i % 2 == 0 else i + 2) < 16
        ],
    )

    packed = jnp.arange(COLS, dtype=jnp.int32)
    per_group = COLS // GROUPS
    group, within = packed // per_group, packed % per_group
    head_at = group * QPER + jnp.minimum(within, QPER - 1)
    heads = jnp.arange(group_heads.shape[0], dtype=jnp.int32)
    head = jnp.sum(jnp.where(head_at[:, None] == heads, group_heads, 0), axis=1)
    n_heads = group_heads.shape[0]
    column = jnp.where(
        within < QPER, head, jnp.where(within == QPER, n_heads + group, n_heads + GROUPS + group)
    )
    earlier = (block_owner[None, :] == block_owner[:, None]) & (packed[None, :] < packed[:, None])
    spot = block_owner * SCAP + jnp.sum(earlier.astype(jnp.int32), axis=1)
    spots = jnp.arange(8 * SCAP, dtype=jnp.int32)
    table = jnp.sum(jnp.where(spots[:, None] == spot[None, :], column + 1, 0), axis=1) - 1
    out = pack(
        jnp.concatenate([odd[None], table]).astype(jnp.int32), keep3, got3, got1, got2
    )
    got = lax.all_to_all(out, "serve", split_axis=0, concat_axis=0, tiled=True)
    turns = jnp.arange(8, dtype=jnp.int32)
    parts = split((me % 8) ^ turns, got)
    landed = [
        send(parts[j], [(i, 2 * ((i % 8) ^ j) + i // 8) for i in ranks]) for j in range(8)
    ]
    served_blocks, tails = place((me // 2) ^ turns, landed)
    served_scales = tails[0::2, :SCAP, 0].T[None]
    return new_master, new_moment, new_variance, served_blocks, served_scales


def solution(mesh):
    state = P("serve", "dp", None, None)
    return jax.shard_map(
        shards,
        mesh=mesh,
        in_specs=(P("dp", "serve"), P("dp", None), state, state, state, P(), P(), P()),
        out_specs=(state, state, state, P("serve", None, "dp", None), P("serve", None, "dp")),
        check_vma=False,
    )
```

```python
import jax
import jax.numpy as jnp
from jax import lax
from jax.experimental import pallas as pl
from jax.experimental.pallas import tpu as pltpu
from jax.sharding import Mesh
from jax.sharding import PartitionSpec as P

QPER = 16
GROUPS = 2
BLK = 128
HALF = 64
UNIT = 9
WIDE = UNIT * BLK
FIRST = 10 * BLK
LAST = 8 * BLK
TILE = 256
CAP = 36
COLS = 36
SCAP = 9
PIECE = 32
MSG = SCAP * PIECE + 16

first_bias = 1.0 - 0.9**10
second_bias = 1.0 - 0.95**10

BF = jnp.bfloat16
F32 = jnp.float32


def cost(flops, nbytes):
    return pl.CostEstimate(flops=flops, bytes_accessed=nbytes, transcendentals=0)


def params(mib=20):
    return pltpu.CompilerParams(vmem_limit_bytes=mib * 1024 * 1024)


def mm_products(refs):
    left = jnp.concatenate([ref[...] for ref in refs[:4]], axis=1)
    for n, right in enumerate(refs[4:]):
        prod = lax.dot_general(
            left, right[...], (((0,), (0,)), ((), ())), preferred_element_type=F32
        ).astype(BF)
        for u in range(4):
            yield u, slice(n * TILE, (n + 1) * TILE), prod[u * BLK : (u + 1) * BLK]


def mm_send_body(table, *refs):
    fwd, bwd = refs[-2:]
    for u, lanes, prod in mm_products(refs[:-2]):
        (fwd if u < 2 else bwd)[u % 2, :, lanes] = prod


def mm_rest_body(table, *refs):
    for u, lanes, prod in mm_products(refs[:-1]):
        refs[-1][u, :, lanes] = prod


def mm(table, inputs, cotangent, part, flip=None):
    tok = inputs.shape[0]
    left = lambda n: pl.BlockSpec((tok, BLK), lambda g, t: (0, t[n, g]))
    right = lambda n: pl.BlockSpec((tok, TILE), lambda g, t: (0, t[4, g] + n))
    tiles = part // TILE
    if flip is None:
        out_specs = pl.BlockSpec((4, BLK, part), lambda g, t: (g, 0, 0))
        out_shape = jax.ShapeDtypeStruct((8, BLK, part), BF)
    else:
        out_specs = [
            pl.BlockSpec((2, BLK, part), lambda g, t: (g, 0, 0)),
            pl.BlockSpec((2, BLK, part), lambda g, t: ((1 - g) if flip else g, 0, 0)),
        ]
        out_shape = [jax.ShapeDtypeStruct((4, BLK, part), BF)] * 2
    return pl.pallas_call(
        mm_rest_body if flip is None else mm_send_body,
        grid_spec=pltpu.PrefetchScalarGridSpec(
            num_scalar_prefetch=1,
            grid=(2,),
            in_specs=[left(n) for n in range(4)] + [right(n) for n in range(tiles)],
            out_specs=out_specs,
        ),
        out_shape=out_shape,
        compiler_params=params(60),
        cost_estimate=cost(2 * 2 * 512 * part * tok, 2 * (tok * (part + 512) + 512 * part) * 2),
        name="gradient_pieces" if flip is None else "gradient_to_send",
    )(table, *([inputs] * 4), *([cotangent] * tiles))


def total(*parts):
    out = parts[0].astype(F32)
    for part in parts[1:]:
        out = out + part.astype(F32)
    return out.astype(BF)


def pair_spec(part, group):
    return pl.BlockSpec((2, BLK, part), lambda s: (group, 0, 0))


def relay_body(to_fwd, to_bwd, fwd, bwd, earlier, out_fwd, out_bwd):
    out_fwd[...] = total(to_fwd[...], fwd[...])
    out_bwd[...] = total(to_bwd[...], bwd[...])


def relay(rest, groups, fwd, bwd, earlier):
    part = rest.shape[2]
    return pl.pallas_call(
        relay_body,
        grid=(1,),
        in_specs=[pair_spec(part, g) for g in (groups[0], groups[1], 0, 0)]
        + [pl.BlockSpec(memory_space=pl.ANY)],
        out_specs=[pair_spec(part, 0)] * 2,
        out_shape=[jax.ShapeDtypeStruct((2, BLK, part), BF)] * 2,
        compiler_params=params(),
        cost_estimate=cost(4 * BLK * part, 12 * BLK * part * 2),
        name="relay_sums",
    )(rest, rest, fwd, bwd, earlier)


def long_sum_body(own_even, own_odd, fwd2, bwd2, fwd, bwd, e0, e1, e2, e3):
    for n, (near, far) in enumerate(((e0, e2), (e1, e3))):
        own, second, first = ((own_even, fwd2, bwd), (own_odd, bwd2, fwd))[n]
        near[...] = total(own[0], second[0], first[0])
        far[...] = total(own[1], second[1], first[1])


def long_sum(rest, groups, fwd2, bwd2, fwd, bwd):
    part = rest.shape[2]
    return pl.pallas_call(
        long_sum_body,
        grid=(1,),
        in_specs=[pair_spec(part, g) for g in (groups[0], groups[1], 0, 0, 1, 1)],
        out_specs=[pl.BlockSpec((BLK, part), lambda s: (0, 0))] * 4,
        out_shape=[jax.ShapeDtypeStruct((BLK, part), BF)] * 4,
        compiler_params=params(),
        cost_estimate=cost(8 * BLK * part, 16 * BLK * part * 2),
        name="long_sums",
    )(rest, rest, fwd2, bwd2, fwd, bwd)


def front_body(own, near, far, other, out, tenth):
    part = total(own[...], near[...], far[...], other[...])
    out[...] = part[:, :WIDE]
    tenth[...] = part[:, WIDE:]


def back_body(own, near, far, other, tenth, out):
    out[:, :BLK] = tenth[...]
    out[:, BLK:] = total(own[...], near[...], far[...], other[...])


def slice_half(body, out_widths, *parts):
    return pl.pallas_call(
        body,
        out_shape=[jax.ShapeDtypeStruct((BLK, w), BF) for w in out_widths],
        compiler_params=params(),
        cost_estimate=cost(4 * BLK * WIDE, 7 * BLK * WIDE * 2),
        name="slice_half",
    )(*parts)


def adam_step(old, moment, variance, grad):
    mom = 0.9 * moment + 0.1 * grad
    var = 0.95 * variance + 0.05 * (grad * grad)
    new = old - 0.02 * (
        (mom * (1.0 / first_bias)) / (jnp.sqrt(var * (1.0 / second_bias)) + 1e-08) + 0.1 * old
    )
    return new, mom, var


def unit_of(place):
    unit = lax.div(place, UNIT)
    return unit, pl.ds(pl.multiple_of((place - unit * UNIT) * BLK, BLK), BLK)


def wrap(slot):
    slot = jnp.where(slot < 0, slot + CAP, slot)
    return jnp.where(slot >= CAP, slot - CAP, slot)


def code_body(units, info, first, second, master, moment, variance, mine, other, scales):
    off, length, odd = info[0], info[1], info[2]
    for n, (unit, grads) in enumerate(zip(units, (first, second))):
        for b in range(UNIT):
            slot = wrap(unit * UNIT + b - off)
            live = slot < length
            lanes = slice(b * BLK, (b + 1) * BLK)
            grad = grads[:, lanes].astype(F32)
            new, _, _ = adam_step(master[0, slot], moment[0, slot], variance[0, slot], grad)
            peak = jnp.max(jnp.abs(new), axis=(0, 1), keepdims=True)
            scale = (peak + 1e-06).astype(BF).astype(F32)
            code = jnp.where(live, new * (1.0 / scale), 0.0).astype(BF)
            top, low = code[:HALF], code[HALF:]
            mine[n, :, lanes] = jnp.where(odd == 1, low, top)
            other[n, :, lanes] = jnp.where(odd == 1, top, low)
            scales[n, :, lanes] = jnp.broadcast_to(jnp.where(live, scale, 0.0), (8, BLK))


def scale_rows(scales, rows):
    return jnp.concatenate(
        [scales[n, 0:1] for n in rows] + [jnp.zeros((16 - len(rows), WIDE), F32)], axis=0
    ).astype(BF)


def own_body(info, a, b, master, moment, variance, keep, send, mine, other, scales):
    code_body((1, 2), info, a, b, master, moment, variance, mine, other, scales)
    tail = scale_rows(scales, (0, 1))
    for ref, held in ((keep, mine), (send, other)):
        ref[:HALF] = held[0]
        ref[HALF : 2 * HALF] = held[1]
        ref[2 * HALF :] = tail


def halo_body(
    info, before, after, master, moment, variance, keep, send, near, far, mine, other, scales
):
    code_body((0, 3), info, before, after, master, moment, variance, mine, other, scales)
    tails = [scale_rows(scales, (n,)) for n in range(2)]

    def write(inside):
        cross = 1 - inside
        keep[:HALF] = mine[inside]
        keep[HALF:] = tails[inside]
        send[:HALF] = other[inside]
        send[HALF:] = tails[inside]
        near[:HALF] = other[cross]
        near[HALF:] = tails[cross]
        far[:HALF] = mine[cross]
        far[HALF:] = tails[cross]

    pl.when(info[2] == 0)(lambda: write(1))
    pl.when(info[2] == 1)(lambda: write(0))


def codes(body, n_out, rows, name, info, a, b, master, moment, variance):
    whole = lambda v: pl.BlockSpec(v.shape, lambda s, t: (0,) * v.ndim)
    return pl.pallas_call(
        body,
        grid_spec=pltpu.PrefetchScalarGridSpec(
            num_scalar_prefetch=1,
            grid=(1,),
            in_specs=[whole(v) for v in (a, b, master, moment, variance)],
            out_specs=[pl.BlockSpec((rows, WIDE), lambda s, t: (0, 0))] * n_out,
            scratch_shapes=[
                pltpu.VMEM((2, HALF, WIDE), BF),
                pltpu.VMEM((2, HALF, WIDE), BF),
                pltpu.VMEM((2, 8, WIDE), F32),
            ],
        ),
        out_shape=[jax.ShapeDtypeStruct((rows, WIDE), BF)] * n_out,
        compiler_params=params(),
        cost_estimate=cost(18 * 16384 * 30, 36 * 16384 * 12),
        name=name,
    )(info, a, b, master, moment, variance)


def state_body(
    info, halo_b, grad_a, grad_b, halo_a, master, moment, variance,
    new_master, new_moment, new_variance, window,
):
    step = pl.program_id(0)
    off, length = info[0], info[1]

    @pl.when(step == 0)
    def _():
        for q, ref in enumerate((halo_b, grad_a, grad_b, halo_a)):
            window[q] = ref[...]

    for n in range(4):
        slot = step * 4 + n
        unit, lanes = unit_of(wrap(off + slot))
        grad = jnp.where(slot < length, window[unit, :, lanes].astype(F32), 0.0)
        new_master[0, n], new_moment[0, n], new_variance[0, n] = adam_step(
            master[0, n], moment[0, n], variance[0, n], grad
        )


def update_state(info, halo_b, grad_a, grad_b, halo_a, master, moment, variance):
    state = pl.BlockSpec((1, 4, BLK, BLK), lambda s, t: (0, s, 0, 0))
    return pl.pallas_call(
        state_body,
        grid_spec=pltpu.PrefetchScalarGridSpec(
            num_scalar_prefetch=1,
            grid=(CAP // 4,),
            in_specs=[pl.BlockSpec((BLK, WIDE), lambda s, t: (0, 0))] * 4 + [state] * 3,
            out_specs=[state] * 3,
            scratch_shapes=[pltpu.VMEM((4, BLK, WIDE), BF)],
        ),
        out_shape=[jax.ShapeDtypeStruct(master.shape, F32)] * 3,
        compiler_params=params(),
        cost_estimate=cost(36 * 16384 * 20, 36 * 16384 * 26),
        name="update_state",
    )(info, halo_b, grad_a, grad_b, halo_a, master, moment, variance)


def pack_body(info, keep2, got2, keep1, got1, near, far, out, row, tails):
    def half(ref, n):
        return ref[n * HALF : (n + 1) * HALF]

    def tail(ref, n):
        at = ref.shape[0] - 16
        return ref[at:].astype(F32)[n : n + 1]

    own, pair = [(keep2, 0), (keep2, 1)], [(got2, 0), (got2, 1)]
    inner_own, inner_pair, by, on = (keep1, 0), (got1, 0), (near, 0), (far, 0)

    def fill(units):
        for q, parts in enumerate(units):
            (a, m), (b, n) = parts
            row[q] = half(a, m) + half(b, n)
            tails[q, 0:1] = tail(a, m) + tail(b, n)

    @pl.when(info[0] == 0)
    def _():
        fill(((own[0], by), (own[1], inner_pair), (pair[0], inner_own), (pair[1], on)))

    @pl.when(info[0] == 1)
    def _():
        fill(((pair[0], on), (pair[1], inner_own), (own[0], inner_pair), (own[1], by)))

    def owner(o, carry):
        rows = []
        for t in range(SCAP):
            col = info[1 + o * SCAP + t]
            unit, lanes = unit_of(jnp.maximum(col, 0))
            piece = row[unit, :, lanes]
            piece = jnp.where(col >= 0, piece, jnp.zeros_like(piece))
            for part in range(2):
                out[2 * o + part, t * PIECE : (t + 1) * PIECE] = piece[
                    part * PIECE : (part + 1) * PIECE
                ]
            rows.append(jnp.where(col >= 0, tails[unit, :, lanes][0:1], 0.0))
        rows.append(jnp.zeros((16 - SCAP, BLK), F32))
        last = jnp.concatenate(rows, axis=0).astype(BF)
        for part in range(2):
            out[2 * o + part, SCAP * PIECE :] = last
        return carry

    lax.fori_loop(0, 8, owner, 0)


def pack(info, *parts):
    return pl.pallas_call(
        pack_body,
        grid_spec=pltpu.PrefetchScalarGridSpec(
            num_scalar_prefetch=1,
            grid=(1,),
            in_specs=[pl.BlockSpec(a.shape, lambda s, t: (0, 0)) for a in parts],
            out_specs=pl.BlockSpec((16, MSG, BLK), lambda s, t: (0, 0, 0)),
            scratch_shapes=[pltpu.VMEM((4, HALF, WIDE), BF), pltpu.VMEM((4, 8, WIDE), F32)],
        ),
        out_shape=jax.ShapeDtypeStruct((16, MSG, BLK), BF),
        compiler_params=params(),
        cost_estimate=cost(0, 3 * 16 * MSG * BLK * 2),
        name="pack_by_owner",
    )(info, *parts)


def place_body(got, out, tails):
    for src in range(16):
        upper, low, x = src // 8, src // 4 % 2, src % 4
        at = (2 * low + x // 2) * BLK + (x % 2) * HALF + upper * PIECE
        for t in range(SCAP):
            out[0, t, at : at + PIECE] = got[src, t * PIECE : (t + 1) * PIECE]
    for q in range(4):
        tails[q] = got[2 * q, SCAP * PIECE :]


def place(got):
    return pl.pallas_call(
        place_body,
        out_shape=[
            jax.ShapeDtypeStruct((1, SCAP, 8 * HALF, BLK), BF),
            jax.ShapeDtypeStruct((4, 16, BLK), BF),
        ],
        compiler_params=params(),
        cost_estimate=cost(0, 2 * 16 * MSG * BLK * 2),
        name="place_served",
    )(got)


def shards(inputs, cotangent, master, moment, variance, slice_start, block_owner, group_heads):
    me = lax.axis_index(("yh", "yl", "x")).astype(jnp.int32)
    y, x = me // 4, me % 4
    ranks = range(16)

    def along_x(k):
        return [(i, i // 4 * 4 + (i + k) % 4) for i in ranks]

    def along_y(k):
        return [(i, (i + 4 * k) % 16) for i in ranks]

    def send(v, pairs):
        return lax.ppermute(v, ("yh", "yl", "x"), pairs)

    def first(k, half):
        to_x = (x + k) % 4
        rows = [2 * ((y + j) % 4) + to_x // 2 for j in (half, half + 2)]
        return rows, (to_x % 2) * 9

    def last(k, half):
        to_y = (y + k) % 4
        tos = [(x + j) % 4 for j in (half, half + 2)]
        return [2 * to_y + t // 2 for t in tos], (tos[0] % 2) * 9 + 5

    def pieces(part, steps, flip=None):
        columns = [g0[0] + g1[0] + [g0[1]] for g0, g1 in steps]
        table = jnp.stack([jnp.stack(c) for c in columns], axis=1)
        return mm(table.astype(jnp.int32), inputs, cotangent, part, flip)

    def long_start(part, groups, flip, along):
        fwd, bwd = pieces(part, groups, flip)
        return send(fwd, along(1)), send(bwd, along(-1))

    a_fwd, a_bwd = long_start(
        FIRST, ((first(2, 0), first(2, 1)), (first(1, 1), first(3, 0))), False, along_x
    )
    b_fwd, b_bwd = long_start(
        LAST, ((last(2, 0), last(3, 0)), (last(1, 1), last(2, 1))), True, along_y
    )
    rest_a = pieces(FIRST, ((first(0, 0), first(0, 1)), (first(1, 0), first(3, 1))))
    rest_b = pieces(LAST, ((last(0, 0), last(1, 0)), (last(0, 1), last(3, 1))))

    def long_end(rest, out_groups, own_groups, fwd, bwd, along, earlier):
        fwd2, bwd2 = relay(rest, out_groups, fwd, bwd, earlier)
        return long_sum(
            rest, own_groups, send(fwd2, along(1)), send(bwd2, along(-1)), fwd, bwd
        )

    part_a = long_end(rest_a, (2, 3), (0, 1), a_fwd, a_bwd, along_x, rest_b)
    part_b = long_end(rest_b, (1, 3), (0, 2), b_fwd, b_bwd, along_y, rest_a)

    def short(parts, along):
        return [parts[0]] + [send(parts[k], along(k)) for k in (2, 1, 3)]

    grad_a, tenth = slice_half(front_body, (WIDE, BLK), *short(part_a, along_y))
    (grad_b,) = slice_half(back_body, (WIDE,), *short(part_b, along_x), tenth)
    halo_a = send(grad_a, [(i + 1, i) for i in range(15)])
    halo_b = send(grad_b, [(i, i + 1) for i in range(15)])

    flat = 16 * 18
    ends = jnp.concatenate([slice_start[1:], jnp.full((1,), flat, jnp.int32)])
    is_me = jnp.arange(16, dtype=jnp.int32) == me
    start = jnp.sum(jnp.where(is_me, slice_start, 0))
    end = jnp.sum(jnp.where(is_me, ends, 0))
    odd = x % 2
    info = jnp.stack([start - (18 * me - 9), end - start, odd]).astype(jnp.int32)
    state = (master, moment, variance)
    keep2, send2 = codes(
        own_body, 2, 2 * HALF + 16, "codes_of_own", info, grad_a, grad_b, *state
    )
    got2 = send(send2, [(i, i ^ 1) for i in ranks])
    keep1, send1, near, far = codes(
        halo_body, 4, HALF + 16, "codes_of_halo", info, halo_b, halo_a, *state
    )
    got1 = send(send1, [(i, i ^ 1) for i in ranks])
    steps = [(i, -1 if i % 2 == 0 else 1) for i in ranks]
    near = send(near, [(i, i + d) for i, d in steps if 0 <= i + d < 16])
    far = send(far, [(i, i + 2 * d) for i, d in steps if 0 <= i + 2 * d < 16])

    packed = jnp.arange(COLS, dtype=jnp.int32)
    per_group = COLS // GROUPS
    group, within = packed // per_group, packed % per_group
    head_at = group * QPER + jnp.minimum(within, QPER - 1)
    heads = jnp.arange(group_heads.shape[0], dtype=jnp.int32)
    head = jnp.sum(jnp.where(head_at[:, None] == heads, group_heads, 0), axis=1)
    n_heads = group_heads.shape[0]
    column = jnp.where(
        within < QPER, head, jnp.where(within == QPER, n_heads + group, n_heads + GROUPS + group)
    )
    earlier = (block_owner[None, :] == block_owner[:, None]) & (packed[None, :] < packed[:, None])
    spot = block_owner * SCAP + jnp.sum(earlier.astype(jnp.int32), axis=1)
    spots = jnp.arange(8 * SCAP, dtype=jnp.int32)
    table = jnp.sum(jnp.where(spots[:, None] == spot[None, :], column + 1, 0), axis=1) - 1
    pack_info = jnp.concatenate([odd[None], table]).astype(jnp.int32)
    out = pack(pack_info, keep2, got2, keep1, got1, near, far)
    out, info = lax.optimization_barrier((out, info))
    new_master, new_moment, new_variance = update_state(
        info, halo_b, grad_a, grad_b, halo_a, *state
    )
    got = lax.all_to_all(out, ("z", "core", "yh"), split_axis=0, concat_axis=0, tiled=True)
    got = lax.all_to_all(got, ("yh", "yl", "x"), split_axis=0, concat_axis=0, tiled=True)
    served_blocks, tails = place(got)
    served_scales = tails[:, :SCAP, 0].T[None]
    return new_master, new_moment, new_variance, served_blocks, served_scales


def solution(mesh):
    dp, serve = ("yh", "yl", "x"), ("z", "core")
    mesh = Mesh(mesh.devices.reshape(2, 2, 4, 4, 2), dp + serve)
    state = P(serve, dp, None, None)
    return jax.shard_map(
        shards,
        mesh=mesh,
        in_specs=(P(dp, serve), P(dp, None), state, state, state, P(), P(), P()),
        out_specs=(state, state, state, P(serve, None, dp, None), P(serve, None, dp)),
        check_vma=False,
    )
```

```python
import functools

import jax
import jax.numpy as jnp
from jax import lax
from jax.experimental import pallas as pl
from jax.experimental.pallas import tpu as pltpu
from jax.sharding import Mesh
from jax.sharding import PartitionSpec as P

QPER = 16
GROUPS = 2
BLK = 128
HALF = 64
UNIT = 9
WIDE = UNIT * BLK
FIRST = 10 * BLK
LAST = 8 * BLK
TILE = 256
CAP = 36
COLS = 36
SCAP = 9
PIECE = 32
MSG = SCAP * PIECE + 16

first_bias = 1.0 - 0.9**10
second_bias = 1.0 - 0.95**10

BF = jnp.bfloat16
F32 = jnp.float32


def cost(flops, nbytes):
    return pl.CostEstimate(flops=flops, bytes_accessed=nbytes, transcendentals=0)


def params(mib=20):
    return pltpu.CompilerParams(vmem_limit_bytes=mib * 1024 * 1024)


def mm_products(refs):
    left = jnp.concatenate([ref[...] for ref in refs[:4]], axis=1)
    for n, right in enumerate(refs[4:]):
        prod = lax.dot_general(
            left, right[...], (((0,), (0,)), ((), ())), preferred_element_type=F32
        ).astype(BF)
        for u in range(4):
            yield u, slice(n * TILE, (n + 1) * TILE), prod[u * BLK : (u + 1) * BLK]


def mm_send_body(tiles, spot, *refs):
    fwd, bwd = refs[-2:]
    for u, lanes, prod in mm_products(refs[: 4 + tiles]):
        (fwd if u < 2 else bwd)[u % 2, :, lanes] = prod


def mm_rest_body(spot, *refs):
    for u, lanes, prod in mm_products(refs[:-1]):
        refs[-1][u, :, lanes] = prod


def mm(spot, which, steps, inputs, cotangent, flip=None):
    tok = inputs.shape[0]
    part = FIRST if which == 0 else LAST
    tiles = part // TILE

    def spread(n, g, t):
        (k0, j0), (k1, j1) = steps[0][n], steps[1][n]
        k, j = jnp.where(g == 0, k0, k1), jnp.where(g == 0, j0, j1)
        dx, dy = (k, j) if which == 0 else (j, k)
        return (t[0] + dx) & 3, (t[1] + dy) & 3

    def left(n):
        def at(g, t):
            to_x, to_y = spread(n, g, t)
            return 0, 2 * to_y + (to_x >> 1)

        return pl.BlockSpec((tok, BLK), at)

    def right(n):
        def at(g, t):
            to_x, _ = spread(0, g, t)
            return 0, (to_x & 1) * 9 + (0 if which == 0 else FIRST // TILE) + n

        return pl.BlockSpec((tok, TILE), at)

    if flip is None:
        out_specs = pl.BlockSpec((4, BLK, part), lambda g, t: (g, 0, 0))
        out_shape = jax.ShapeDtypeStruct((8, BLK, part), BF)
    else:
        out_specs = [
            pl.BlockSpec((2, BLK, part), lambda g, t: (g, 0, 0)),
            pl.BlockSpec((2, BLK, part), lambda g, t: ((1 - g) if flip else g, 0, 0)),
        ]
        out_shape = [jax.ShapeDtypeStruct((4, BLK, part), BF)] * 2
    return pl.pallas_call(
        mm_rest_body if flip is None else functools.partial(mm_send_body, tiles),
        grid_spec=pltpu.PrefetchScalarGridSpec(
            num_scalar_prefetch=1,
            grid=(2,),
            in_specs=[left(n) for n in range(4)] + [right(n) for n in range(tiles)],
            out_specs=out_specs,
        ),
        out_shape=out_shape,
        compiler_params=params(60),
        cost_estimate=cost(2 * 2 * 512 * part * tok, 2 * (tok * (part + 512) + 512 * part) * 2),
        name="gradient_pieces" if flip is None else "gradient_to_send",
    )(spot, *([inputs] * 4), *([cotangent] * tiles))


def total(*parts):
    out = parts[0].astype(F32)
    for part in parts[1:]:
        out = out + part.astype(F32)
    return out.astype(BF)


def pair_spec(part, group):
    return pl.BlockSpec((2, BLK, part), lambda s: (group, 0, 0))


def relay_body(to_fwd, to_bwd, fwd, bwd, *refs):
    out_fwd, out_bwd = refs[-2:]
    out_fwd[...] = total(to_fwd[...], fwd[...])
    out_bwd[...] = total(to_bwd[...], bwd[...])


def relay(rest, groups, fwd, bwd, earlier):
    part = rest.shape[2]
    return pl.pallas_call(
        relay_body,
        grid=(1,),
        in_specs=[pair_spec(part, g) for g in (groups[0], groups[1], 0, 0)]
        + [pl.BlockSpec(memory_space=pl.ANY)] * len(earlier),
        out_specs=[pair_spec(part, 0)] * 2,
        out_shape=[jax.ShapeDtypeStruct((2, BLK, part), BF)] * 2,
        compiler_params=params(),
        cost_estimate=cost(4 * BLK * part, 12 * BLK * part * 2),
        name="relay_sums",
    )(rest, rest, fwd, bwd, *earlier)


def long_sum_body(own_even, own_odd, fwd2, bwd2, fwd, bwd, e0, e1, e2, e3):
    for n, (near, far) in enumerate(((e0, e2), (e1, e3))):
        own, second, first = ((own_even, fwd2, bwd), (own_odd, bwd2, fwd))[n]
        near[...] = total(own[0], second[0], first[0])
        far[...] = total(own[1], second[1], first[1])


def long_sum(rest, groups, fwd2, bwd2, fwd, bwd):
    part = rest.shape[2]
    return pl.pallas_call(
        long_sum_body,
        grid=(1,),
        in_specs=[pair_spec(part, g) for g in (groups[0], groups[1], 0, 0, 1, 1)],
        out_specs=[pl.BlockSpec((BLK, part), lambda s: (0, 0))] * 4,
        out_shape=[jax.ShapeDtypeStruct((BLK, part), BF)] * 4,
        compiler_params=params(),
        cost_estimate=cost(8 * BLK * part, 16 * BLK * part * 2),
        name="long_sums",
    )(rest, rest, fwd2, bwd2, fwd, bwd)


def slice_body(info, *refs):
    front, back, to_pair, to_cross = refs[8:]
    first = total(*(ref[...] for ref in refs[:4]))
    last = total(*(ref[...] for ref in refs[4:8]))
    front[...] = first[:, :WIDE]
    back[:, :BLK] = first[:, WIDE:]
    back[:, BLK:] = last

    @pl.when(info[2] == 0)
    def _():
        to_pair[...] = back[...]
        to_cross[...] = front[...]

    @pl.when(info[2] == 1)
    def _():
        to_pair[...] = front[...]
        to_cross[...] = back[...]


def slices(info, *parts):
    return pl.pallas_call(
        slice_body,
        grid_spec=pltpu.PrefetchScalarGridSpec(
            num_scalar_prefetch=1,
            grid=(1,),
            in_specs=[pl.BlockSpec(v.shape, lambda s, t: (0, 0)) for v in parts],
            out_specs=[pl.BlockSpec((BLK, WIDE), lambda s, t: (0, 0))] * 4,
        ),
        out_shape=[jax.ShapeDtypeStruct((BLK, WIDE), BF)] * 4,
        compiler_params=params(),
        cost_estimate=cost(8 * BLK * WIDE, 12 * BLK * WIDE * 2),
        name="slices",
    )(info, *parts)


def adam_step(old, moment, variance, grad):
    mom = 0.9 * moment + 0.1 * grad
    var = 0.95 * variance + 0.05 * (grad * grad)
    new = old - 0.02 * (
        (mom * (1.0 / first_bias)) / (jnp.sqrt(var * (1.0 / second_bias)) + 1e-08) + 0.1 * old
    )
    return new, mom, var


def unit_of(place):
    unit = lax.div(place, UNIT)
    return unit, pl.ds(pl.multiple_of((place - unit * UNIT) * BLK, BLK), BLK)


def wrap(slot):
    slot = jnp.where(slot < 0, slot + CAP, slot)
    return jnp.where(slot >= CAP, slot - CAP, slot)


def code_body(units, info, first, second, master, moment, variance, mine, other, scales):
    off, length, odd = info[0], info[1], info[2]
    for n, (unit, grads) in enumerate(zip(units, (first, second))):
        for b in range(UNIT):
            slot = wrap(unit * UNIT + b - off)
            live = slot < length
            lanes = slice(b * BLK, (b + 1) * BLK)
            grad = grads[:, lanes].astype(F32)
            new, _, _ = adam_step(master[0, slot], moment[0, slot], variance[0, slot], grad)
            peak = jnp.max(jnp.abs(new), axis=(0, 1), keepdims=True)
            scale = (peak + 1e-06).astype(BF).astype(F32)
            code = jnp.where(live, new * (1.0 / scale), 0.0).astype(BF)
            top, low = code[:HALF], code[HALF:]
            mine[n, :, lanes] = jnp.where(odd == 1, low, top)
            other[n, :, lanes] = jnp.where(odd == 1, top, low)
            scales[n, :, lanes] = jnp.broadcast_to(jnp.where(live, scale, 0.0), (8, BLK))


def scale_rows(scales, rows):
    return jnp.concatenate(
        [scales[n, 0:1] for n in rows] + [jnp.zeros((16 - len(rows), WIDE), F32)], axis=0
    ).astype(BF)


def own_body(info, a, b, master, moment, variance, keep, send, mine, other, scales):
    code_body((1, 2), info, a, b, master, moment, variance, mine, other, scales)
    tail = scale_rows(scales, (0, 1))
    for ref, held in ((keep, mine), (send, other)):
        ref[:HALF] = held[0]
        ref[HALF : 2 * HALF] = held[1]
        ref[2 * HALF :] = tail


def halo_body(
    info, inside, cross, master, moment, variance, keep, send, near, far, mine, other, scales
):
    odd = info[2]
    units = (3 - 3 * odd, 3 * odd)
    code_body(units, info, inside, cross, master, moment, variance, mine, other, scales)
    for n, outs in enumerate(((keep, send), (far, near))):
        tail = scale_rows(scales, (n,))
        for ref, held in zip(outs, (mine, other)):
            ref[:HALF] = held[n]
            ref[HALF:] = tail


def codes(body, n_out, rows, name, info, a, b, master, moment, variance):
    whole = lambda v: pl.BlockSpec(v.shape, lambda s, t: (0,) * v.ndim)
    return pl.pallas_call(
        body,
        grid_spec=pltpu.PrefetchScalarGridSpec(
            num_scalar_prefetch=1,
            grid=(1,),
            in_specs=[whole(v) for v in (a, b, master, moment, variance)],
            out_specs=[pl.BlockSpec((rows, WIDE), lambda s, t: (0, 0))] * n_out,
            scratch_shapes=[
                pltpu.VMEM((2, HALF, WIDE), BF),
                pltpu.VMEM((2, HALF, WIDE), BF),
                pltpu.VMEM((2, 8, WIDE), F32),
            ],
        ),
        out_shape=[jax.ShapeDtypeStruct((rows, WIDE), BF)] * n_out,
        compiler_params=params(),
        cost_estimate=cost(18 * 16384 * 30, 36 * 16384 * 12),
        name=name,
    )(info, a, b, master, moment, variance)


def state_body(
    info, inside, front, back, cross, master, moment, variance,
    new_master, new_moment, new_variance, window,
):
    step = pl.program_id(0)
    off, length = info[0], info[1]

    @pl.when(step == 0)
    def _():
        window[1] = front[...]
        window[2] = back[...]
        window[3 - 3 * info[2]] = inside[...]
        window[3 * info[2]] = cross[...]

    for n in range(4):
        slot = step * 4 + n
        unit, lanes = unit_of(wrap(off + slot))
        grad = jnp.where(slot < length, window[unit, :, lanes].astype(F32), 0.0)
        new_master[0, n], new_moment[0, n], new_variance[0, n] = adam_step(
            master[0, n], moment[0, n], variance[0, n], grad
        )


def update_state(info, inside, front, back, cross, master, moment, variance):
    state = pl.BlockSpec((1, 4, BLK, BLK), lambda s, t: (0, s, 0, 0))
    return pl.pallas_call(
        state_body,
        grid_spec=pltpu.PrefetchScalarGridSpec(
            num_scalar_prefetch=1,
            grid=(CAP // 4,),
            in_specs=[pl.BlockSpec((BLK, WIDE), lambda s, t: (0, 0))] * 4 + [state] * 3,
            out_specs=[state] * 3,
            scratch_shapes=[pltpu.VMEM((4, BLK, WIDE), BF)],
        ),
        out_shape=[jax.ShapeDtypeStruct(master.shape, F32)] * 3,
        compiler_params=params(),
        cost_estimate=cost(36 * 16384 * 20, 36 * 16384 * 26),
        name="update_state",
    )(info, inside, front, back, cross, master, moment, variance)


def pack_body(info, keep2, got2, keep1, got1, near, far, out, row, tails):
    def half(ref, n):
        return ref[n * HALF : (n + 1) * HALF]

    def tail(ref, n):
        at = ref.shape[0] - 16
        return ref[at:].astype(F32)[n : n + 1]

    own, pair = [(keep2, 0), (keep2, 1)], [(got2, 0), (got2, 1)]
    inner_own, inner_pair, by, on = (keep1, 0), (got1, 0), (near, 0), (far, 0)

    def fill(units):
        for q, parts in enumerate(units):
            (a, m), (b, n) = parts
            row[q] = half(a, m) + half(b, n)
            tails[q, 0:1] = tail(a, m) + tail(b, n)

    @pl.when(info[0] == 0)
    def _():
        fill(((own[0], by), (own[1], inner_pair), (pair[0], inner_own), (pair[1], on)))

    @pl.when(info[0] == 1)
    def _():
        fill(((pair[0], on), (pair[1], inner_own), (own[0], inner_pair), (own[1], by)))

    def owner(o, carry):
        rows = []
        for t in range(SCAP):
            col = info[1 + o * SCAP + t]
            unit, lanes = unit_of(jnp.maximum(col, 0))
            piece = row[unit, :, lanes]
            piece = jnp.where(col >= 0, piece, jnp.zeros_like(piece))
            for part in range(2):
                out[2 * o + part, t * PIECE : (t + 1) * PIECE] = piece[
                    part * PIECE : (part + 1) * PIECE
                ]
            rows.append(jnp.where(col >= 0, tails[unit, :, lanes][0:1], 0.0))
        rows.append(jnp.zeros((16 - SCAP, BLK), F32))
        last = jnp.concatenate(rows, axis=0).astype(BF)
        for part in range(2):
            out[2 * o + part, SCAP * PIECE :] = last
        return carry

    lax.fori_loop(0, 8, owner, 0)


def pack(info, *parts):
    return pl.pallas_call(
        pack_body,
        grid_spec=pltpu.PrefetchScalarGridSpec(
            num_scalar_prefetch=1,
            grid=(1,),
            in_specs=[pl.BlockSpec(a.shape, lambda s, t: (0, 0)) for a in parts],
            out_specs=pl.BlockSpec((16, MSG, BLK), lambda s, t: (0, 0, 0)),
            scratch_shapes=[pltpu.VMEM((4, HALF, WIDE), BF), pltpu.VMEM((4, 8, WIDE), F32)],
        ),
        out_shape=jax.ShapeDtypeStruct((16, MSG, BLK), BF),
        compiler_params=params(),
        cost_estimate=cost(0, 3 * 16 * MSG * BLK * 2),
        name="pack_by_owner",
    )(info, *parts)


def place_body(got, out, scales):
    for src in range(16):
        upper, low, x = src // 8, src // 4 % 2, src % 4
        at = (2 * low + x // 2) * BLK + (x % 2) * HALF + upper * PIECE
        for t in range(SCAP):
            out[0, t, at : at + PIECE] = got[src, t * PIECE : (t + 1) * PIECE]
    lane = lax.broadcasted_iota(jnp.int32, (16, BLK), 1)
    rows = jnp.zeros((16, BLK), F32)
    for q in range(4):
        rows = jnp.where(lane == q, got[2 * q, SCAP * PIECE :].astype(F32), rows)
    scales[0] = rows[:SCAP, :4].astype(BF)


def place(got):
    return pl.pallas_call(
        place_body,
        out_shape=[
            jax.ShapeDtypeStruct((1, SCAP, 8 * HALF, BLK), BF),
            jax.ShapeDtypeStruct((1, SCAP, 4), BF),
        ],
        compiler_params=params(),
        cost_estimate=cost(0, 2 * 16 * MSG * BLK * 2),
        name="place_served",
    )(got)


def shards(inputs, cotangent, master, moment, variance, slice_start, block_owner, group_heads):
    me = lax.axis_index(("yh", "yl", "x")).astype(jnp.int32)
    y, x = me // 4, me % 4
    ranks = range(16)

    def along_x(k):
        return [(i, i // 4 * 4 + (i + k) % 4) for i in ranks]

    def along_y(k):
        return [(i, (i + 4 * k) % 16) for i in ranks]

    def send(v, pairs):
        return lax.ppermute(v, ("yh", "yl", "x"), pairs)

    here = jnp.stack([x, y]).astype(jnp.int32)

    def two(k, half):
        return [(k, half), (k, half + 2)]

    def pieces(which, steps, flip=None):
        return mm(here, which, [g0 + g1 for g0, g1 in steps], inputs, cotangent, flip)

    def long_start(which, groups, flip, along):
        fwd, bwd = pieces(which, groups, flip)
        return send(fwd, along(1)), send(bwd, along(-1))

    a_fwd, a_bwd = long_start(
        0, ((two(2, 0), two(2, 1)), (two(1, 1), two(3, 0))), False, along_x
    )
    b_fwd, b_bwd = long_start(
        1, ((two(2, 0), two(3, 0)), (two(1, 1), two(2, 1))), True, along_y
    )
    rest_a = pieces(0, ((two(0, 0), two(0, 1)), (two(1, 0), two(3, 1))))
    rest_b = pieces(1, ((two(0, 0), two(1, 0)), (two(0, 1), two(3, 1))))

    def long_end(rest, out_groups, own_groups, fwd, bwd, along, earlier):
        fwd2, bwd2 = relay(rest, out_groups, fwd, bwd, earlier)
        return long_sum(
            rest, own_groups, send(fwd2, along(1)), send(bwd2, along(-1)), fwd, bwd
        )

    flat = 16 * 18
    ends = jnp.concatenate([slice_start[1:], jnp.full((1,), flat, jnp.int32)])
    is_me = jnp.arange(16, dtype=jnp.int32) == me
    start = jnp.sum(jnp.where(is_me, slice_start, 0))
    end = jnp.sum(jnp.where(is_me, ends, 0))
    odd = x % 2
    info = jnp.stack([start - (18 * me - 9), end - start, odd]).astype(jnp.int32)

    packed = jnp.arange(COLS, dtype=jnp.int32)
    per_group = COLS // GROUPS
    group, within = packed // per_group, packed % per_group
    head_at = group * QPER + jnp.minimum(within, QPER - 1)
    heads = jnp.arange(group_heads.shape[0], dtype=jnp.int32)
    head = jnp.sum(jnp.where(head_at[:, None] == heads, group_heads, 0), axis=1)
    n_heads = group_heads.shape[0]
    column = jnp.where(
        within < QPER, head, jnp.where(within == QPER, n_heads + group, n_heads + GROUPS + group)
    )
    earlier = (block_owner[None, :] == block_owner[:, None]) & (packed[None, :] < packed[:, None])
    spot = block_owner * SCAP + jnp.sum(earlier.astype(jnp.int32), axis=1)
    spots = jnp.arange(8 * SCAP, dtype=jnp.int32)
    table = jnp.sum(jnp.where(spots[:, None] == spot[None, :], column + 1, 0), axis=1) - 1
    pack_info = jnp.concatenate([odd[None], table]).astype(jnp.int32)

    part_a = long_end(rest_a, (2, 3), (0, 1), a_fwd, a_bwd, along_x,
        (rest_b,),
    )
    part_b = long_end(rest_b, (1, 3), (0, 2), b_fwd, b_bwd, along_y, (rest_a,)
    )

    def short(parts, along):
        return [parts[0]] + [send(parts[k], along(k)) for k in (2, 1, 3)]

    front, back, to_pair, to_cross = slices(
        info, *short(part_a, along_y), *short(part_b, along_x)
    )
    pairs = [(i, i ^ 1) for i in ranks]
    near_by = [(i, i - 1 if i % 2 == 0 else i + 1) for i in ranks if 0 < i < 15]
    far_off = [
        (i, i - 2 if i % 2 == 0 else i + 2)
        for i in ranks
        if 0 <= (i - 2 if i % 2 == 0 else i + 2) < 16
    ]
    inside = send(to_pair, pairs)
    cross = send(to_cross, near_by)

    state = (master, moment, variance)
    keep2, send2 = codes(own_body, 2, 2 * HALF + 16, "codes_of_own", info, front, back, *state)
    got2 = send(send2, pairs)
    keep1, send1, near, far = codes(
        halo_body, 4, HALF + 16, "codes_of_halo", info, inside, cross, *state
    )
    got1 = send(send1, pairs)
    near = send(near, near_by)
    far = send(far, far_off)

    updated = update_state(info, inside, front, back, cross, *state)
    got1, near, far, *updated = lax.optimization_barrier((got1, near, far, *updated))
    out = pack(pack_info, keep2, got2, keep1, got1, near, far)
    got = lax.all_to_all(out, ("z", "core", "yh"), split_axis=0, concat_axis=0, tiled=True)
    got = lax.all_to_all(got, ("yh", "yl", "x"), split_axis=0, concat_axis=0, tiled=True)
    served_blocks, served_scales = place(got)
    return (*updated, served_blocks, served_scales)


def solution(mesh):
    dp, serve = ("yh", "yl", "x"), ("z", "core")
    mesh = Mesh(mesh.devices.reshape(2, 2, 4, 4, 2), dp + serve)
    state = P(serve, dp, None, None)
    return jax.shard_map(
        shards,
        mesh=mesh,
        in_specs=(P(dp, serve), P(dp, None), state, state, state, P(), P(), P()),
        out_specs=(state, state, state, P(serve, None, dp, None), P(serve, None, dp)),
        check_vma=False,
    )
```

```python
import functools

import jax
import jax.numpy as jnp
from jax import lax
from jax.experimental import pallas as pl
from jax.experimental.pallas import tpu as pltpu
from jax.sharding import Mesh
from jax.sharding import PartitionSpec as P

QPER = 16
GROUPS = 2
BLK = 128
HALF = 64
UNIT = 9
WIDE = UNIT * BLK
FIRST = 10 * BLK
LAST = 8 * BLK
TILE = 256
CAP = 36
COLS = 36
SCAP = 9
STEP = 9
PIECE = 32
MSG = SCAP * PIECE + 16

first_bias = 1.0 - 0.9**10
second_bias = 1.0 - 0.95**10

BF = jnp.bfloat16
F32 = jnp.float32


def cost(flops, nbytes):
    return pl.CostEstimate(flops=flops, bytes_accessed=nbytes, transcendentals=0)


def params(mib=20):
    return pltpu.CompilerParams(vmem_limit_bytes=mib * 1024 * 1024)


def mm_products(refs):
    left = jnp.concatenate([ref[...] for ref in refs[:4]], axis=1)
    for n, right in enumerate(refs[4:]):
        prod = lax.dot_general(
            left, right[...], (((0,), (0,)), ((), ())), preferred_element_type=F32
        ).astype(BF)
        for u in range(4):
            yield u, slice(n * TILE, (n + 1) * TILE), prod[u * BLK : (u + 1) * BLK]


def mm_send_body(tiles, spot, *refs):
    fwd, bwd = refs[-2:]
    for u, lanes, prod in mm_products(refs[: 4 + tiles]):
        (fwd if u < 2 else bwd)[u % 2, :, lanes] = prod


def mm_rest_body(spot, *refs):
    for u, lanes, prod in mm_products(refs[:-1]):
        refs[-1][u, :, lanes] = prod


def mm(spot, which, steps, inputs, cotangent, flip=None):
    tok = inputs.shape[0]
    part = FIRST if which == 0 else LAST
    tiles = part // TILE

    def spread(n, g, t):
        (k0, j0), (k1, j1) = steps[0][n], steps[1][n]
        k, j = jnp.where(g == 0, k0, k1), jnp.where(g == 0, j0, j1)
        dx, dy = (k, j) if which == 0 else (j, k)
        return (t[0] + dx) & 3, (t[1] + dy) & 3

    def left(n):
        def at(g, t):
            to_x, to_y = spread(n, g, t)
            return 0, 2 * to_y + (to_x >> 1)

        return pl.BlockSpec((tok, BLK), at)

    def right(n):
        def at(g, t):
            to_x, _ = spread(0, g, t)
            return 0, (to_x & 1) * 9 + (0 if which == 0 else FIRST // TILE) + n

        return pl.BlockSpec((tok, TILE), at)

    if flip is None:
        out_specs = pl.BlockSpec((4, BLK, part), lambda g, t: (g, 0, 0))
        out_shape = jax.ShapeDtypeStruct((8, BLK, part), BF)
    else:
        out_specs = [
            pl.BlockSpec((2, BLK, part), lambda g, t: (g, 0, 0)),
            pl.BlockSpec((2, BLK, part), lambda g, t: ((1 - g) if flip else g, 0, 0)),
        ]
        out_shape = [jax.ShapeDtypeStruct((4, BLK, part), BF)] * 2
    return pl.pallas_call(
        mm_rest_body if flip is None else functools.partial(mm_send_body, tiles),
        grid_spec=pltpu.PrefetchScalarGridSpec(
            num_scalar_prefetch=1,
            grid=(2,),
            in_specs=[left(n) for n in range(4)] + [right(n) for n in range(tiles)],
            out_specs=out_specs,
        ),
        out_shape=out_shape,
        compiler_params=params(60),
        cost_estimate=cost(2 * 2 * 512 * part * tok, 2 * (tok * (part + 512) + 512 * part) * 2),
        name="gradient_pieces" if flip is None else "gradient_to_send",
    )(spot, *([inputs] * 4), *([cotangent] * tiles))


def total(*parts):
    out = parts[0].astype(F32)
    for part in parts[1:]:
        out = out + part.astype(F32)
    return out.astype(BF)


def pair_spec(part, group):
    return pl.BlockSpec((2, BLK, part), lambda s: (group, 0, 0))


def relay_body(to_fwd, to_bwd, fwd, bwd, *refs):
    out_fwd, out_bwd = refs[-2:]
    out_fwd[...] = total(to_fwd[...], fwd[...])
    out_bwd[...] = total(to_bwd[...], bwd[...])


def relay(rest, groups, fwd, bwd, earlier):
    part = rest.shape[2]
    return pl.pallas_call(
        relay_body,
        grid=(1,),
        in_specs=[pair_spec(part, g) for g in (groups[0], groups[1], 0, 0)]
        + [pl.BlockSpec(memory_space=pl.ANY)] * len(earlier),
        out_specs=[pair_spec(part, 0)] * 2,
        out_shape=[jax.ShapeDtypeStruct((2, BLK, part), BF)] * 2,
        compiler_params=params(),
        cost_estimate=cost(4 * BLK * part, 12 * BLK * part * 2),
        name="relay_sums",
    )(rest, rest, fwd, bwd, *earlier)


def long_sum_body(own_even, own_odd, fwd2, bwd2, fwd, bwd, e0, e1, e2, e3):
    for n, (near, far) in enumerate(((e0, e2), (e1, e3))):
        own, second, first = ((own_even, fwd2, bwd), (own_odd, bwd2, fwd))[n]
        near[...] = total(own[0], second[0], first[0])
        far[...] = total(own[1], second[1], first[1])


def long_sum(rest, groups, fwd2, bwd2, fwd, bwd):
    part = rest.shape[2]
    return pl.pallas_call(
        long_sum_body,
        grid=(1,),
        in_specs=[pair_spec(part, g) for g in (groups[0], groups[1], 0, 0, 1, 1)],
        out_specs=[pl.BlockSpec((BLK, part), lambda s: (0, 0))] * 4,
        out_shape=[jax.ShapeDtypeStruct((BLK, part), BF)] * 4,
        compiler_params=params(48),
        cost_estimate=cost(8 * BLK * part, 16 * BLK * part * 2),
        name="long_sums",
    )(rest, rest, fwd2, bwd2, fwd, bwd)


def slice_body(info, *refs):
    front, back, to_pair, to_cross = refs[8:]
    first = total(*(ref[...] for ref in refs[:4]))
    last = total(*(ref[...] for ref in refs[4:8]))
    front[...] = first[:, :WIDE]
    back[:, :BLK] = first[:, WIDE:]
    back[:, BLK:] = last

    @pl.when(info[2] == 0)
    def _():
        to_pair[...] = back[...]
        to_cross[...] = front[...]

    @pl.when(info[2] == 1)
    def _():
        to_pair[...] = front[...]
        to_cross[...] = back[...]


def slices(info, *parts):
    return pl.pallas_call(
        slice_body,
        grid_spec=pltpu.PrefetchScalarGridSpec(
            num_scalar_prefetch=1,
            grid=(1,),
            in_specs=[pl.BlockSpec(v.shape, lambda s, t: (0, 0)) for v in parts],
            out_specs=[pl.BlockSpec((BLK, WIDE), lambda s, t: (0, 0))] * 4,
        ),
        out_shape=[jax.ShapeDtypeStruct((BLK, WIDE), BF)] * 4,
        compiler_params=params(),
        cost_estimate=cost(8 * BLK * WIDE, 12 * BLK * WIDE * 2),
        name="slices",
    )(info, *parts)


def adam_step(old, moment, variance, grad):
    mom = 0.9 * moment + 0.1 * grad
    var = 0.95 * variance + 0.05 * (grad * grad)
    new = old - 0.02 * (
        (mom * (1.0 / first_bias)) / (jnp.sqrt(var * (1.0 / second_bias)) + 1e-08) + 0.1 * old
    )
    return new, mom, var


def unit_of(place):
    unit = lax.div(place, UNIT)
    return unit, pl.ds(pl.multiple_of((place - unit * UNIT) * BLK, BLK), BLK)


def wrap(slot):
    slot = jnp.where(slot < 0, slot + CAP, slot)
    return jnp.where(slot >= CAP, slot - CAP, slot)


def code_body(units, info, first, second, master, moment, variance, mine, other, scales):
    off, length, odd = info[0], info[1], info[2]
    for n, (unit, grads) in enumerate(zip(units, (first, second))):
        for b in range(UNIT):
            slot = wrap(unit * UNIT + b - off)
            live = slot < length
            lanes = slice(b * BLK, (b + 1) * BLK)
            grad = grads[:, lanes].astype(F32)
            new, _, _ = adam_step(master[0, slot], moment[0, slot], variance[0, slot], grad)
            peak = jnp.max(jnp.abs(new), axis=(0, 1), keepdims=True)
            scale = (peak + 1e-06).astype(BF).astype(F32)
            code = jnp.where(live, new * (1.0 / scale), 0.0).astype(BF)
            top, low = code[:HALF], code[HALF:]
            mine[n, :, lanes] = jnp.where(odd == 1, low, top)
            other[n, :, lanes] = jnp.where(odd == 1, top, low)
            scales[n, :, lanes] = jnp.broadcast_to(jnp.where(live, scale, 0.0), (8, BLK))


def scale_rows(scales, rows):
    return jnp.concatenate(
        [scales[n, 0:1] for n in rows] + [jnp.zeros((16 - len(rows), WIDE), F32)], axis=0
    ).astype(BF)


def own_body(info, a, b, master, moment, variance, keep, send, mine, other, scales):
    code_body((1, 2), info, a, b, master, moment, variance, mine, other, scales)
    tail = scale_rows(scales, (0, 1))
    for ref, held in ((keep, mine), (send, other)):
        ref[:HALF] = held[0]
        ref[HALF : 2 * HALF] = held[1]
        ref[2 * HALF :] = tail


def halo_body(
    info, inside, cross, master, moment, variance, keep, send, near, far, mine, other, scales
):
    odd = info[2]
    units = (3 - 3 * odd, 3 * odd)
    code_body(units, info, inside, cross, master, moment, variance, mine, other, scales)
    for n, outs in enumerate(((keep, send), (far, near))):
        tail = scale_rows(scales, (n,))
        for ref, held in zip(outs, (mine, other)):
            ref[:HALF] = held[n]
            ref[HALF:] = tail


def codes(body, n_out, rows, name, info, a, b, master, moment, variance):
    whole = lambda v: pl.BlockSpec(v.shape, lambda s, t: (0,) * v.ndim)
    return pl.pallas_call(
        body,
        grid_spec=pltpu.PrefetchScalarGridSpec(
            num_scalar_prefetch=1,
            grid=(1,),
            in_specs=[whole(v) for v in (a, b, master, moment, variance)],
            out_specs=[pl.BlockSpec((rows, WIDE), lambda s, t: (0, 0))] * n_out,
            scratch_shapes=[
                pltpu.VMEM((2, HALF, WIDE), BF),
                pltpu.VMEM((2, HALF, WIDE), BF),
                pltpu.VMEM((2, 8, WIDE), F32),
            ],
        ),
        out_shape=[jax.ShapeDtypeStruct((rows, WIDE), BF)] * n_out,
        compiler_params=params(),
        cost_estimate=cost(18 * 16384 * 30, 36 * 16384 * 12),
        name=name,
    )(info, a, b, master, moment, variance)


def state_body(
    info, inside, front, back, cross, master, moment, variance,
    new_master, new_moment, new_variance, window,
):
    step = pl.program_id(0)
    off, length = info[0], info[1]

    @pl.when(step == 0)
    def _():
        window[1] = front[...]
        window[2] = back[...]
        window[3 - 3 * info[2]] = inside[...]
        window[3 * info[2]] = cross[...]

    for n in range(STEP):
        slot = step * STEP + n
        unit, lanes = unit_of(wrap(off + slot))
        grad = jnp.where(slot < length, window[unit, :, lanes].astype(F32), 0.0)
        new_master[0, n], new_moment[0, n], new_variance[0, n] = adam_step(
            master[0, n], moment[0, n], variance[0, n], grad
        )


def update_state(info, inside, front, back, cross, master, moment, variance):
    state = pl.BlockSpec((1, STEP, BLK, BLK), lambda s, t: (0, s, 0, 0))
    return pl.pallas_call(
        state_body,
        grid_spec=pltpu.PrefetchScalarGridSpec(
            num_scalar_prefetch=1,
            grid=(CAP // STEP,),
            in_specs=[pl.BlockSpec((BLK, WIDE), lambda s, t: (0, 0))] * 4 + [state] * 3,
            out_specs=[state] * 3,
            scratch_shapes=[pltpu.VMEM((4, BLK, WIDE), BF)],
        ),
        out_shape=[jax.ShapeDtypeStruct(master.shape, F32)] * 3,
        compiler_params=params(32),
        cost_estimate=cost(36 * 16384 * 20, 36 * 16384 * 26),
        name="update_state",
    )(info, inside, front, back, cross, master, moment, variance)


def pack_body(info, keep2, got2, keep1, got1, near, far, out, row, tails):
    def half(ref, n):
        return ref[n * HALF : (n + 1) * HALF]

    def tail(ref, n):
        at = ref.shape[0] - 16
        return ref[at:].astype(F32)[n : n + 1]

    own, pair = [(keep2, 0), (keep2, 1)], [(got2, 0), (got2, 1)]
    inner_own, inner_pair, by, on = (keep1, 0), (got1, 0), (near, 0), (far, 0)

    def fill(units):
        for q, parts in enumerate(units):
            (a, m), (b, n) = parts
            row[q] = half(a, m) + half(b, n)
            tails[q, 0:1] = tail(a, m) + tail(b, n)

    @pl.when(info[0] == 0)
    def _():
        fill(((own[0], by), (own[1], inner_pair), (pair[0], inner_own), (pair[1], on)))

    @pl.when(info[0] == 1)
    def _():
        fill(((pair[0], on), (pair[1], inner_own), (own[0], inner_pair), (own[1], by)))

    def owner(o, carry):
        rows = []
        for t in range(SCAP):
            col = info[1 + o * SCAP + t]
            unit, lanes = unit_of(jnp.maximum(col, 0))
            piece = row[unit, :, lanes]
            piece = jnp.where(col >= 0, piece, jnp.zeros_like(piece))
            for part in range(2):
                out[2 * o + part, t * PIECE : (t + 1) * PIECE] = piece[
                    part * PIECE : (part + 1) * PIECE
                ]
            rows.append(jnp.where(col >= 0, tails[unit, :, lanes][0:1], 0.0))
        rows.append(jnp.zeros((16 - SCAP, BLK), F32))
        last = jnp.concatenate(rows, axis=0).astype(BF)
        for part in range(2):
            out[2 * o + part, SCAP * PIECE :] = last
        return carry

    lax.fori_loop(0, 8, owner, 0)


def pack(info, *parts):
    return pl.pallas_call(
        pack_body,
        grid_spec=pltpu.PrefetchScalarGridSpec(
            num_scalar_prefetch=1,
            grid=(1,),
            in_specs=[pl.BlockSpec(a.shape, lambda s, t: (0, 0)) for a in parts],
            out_specs=pl.BlockSpec((16, MSG, BLK), lambda s, t: (0, 0, 0)),
            scratch_shapes=[pltpu.VMEM((4, HALF, WIDE), BF), pltpu.VMEM((4, 8, WIDE), F32)],
        ),
        out_shape=jax.ShapeDtypeStruct((16, MSG, BLK), BF),
        compiler_params=params(),
        cost_estimate=cost(0, 3 * 16 * MSG * BLK * 2),
        name="pack_by_owner",
    )(info, *parts)


def place_body(got, out, scales):
    for src in range(16):
        upper, low, x = src // 8, src // 4 % 2, src % 4
        at = (2 * low + x // 2) * BLK + (x % 2) * HALF + upper * PIECE
        for t in range(SCAP):
            out[0, t, at : at + PIECE] = got[src, t * PIECE : (t + 1) * PIECE]
    lane = lax.broadcasted_iota(jnp.int32, (16, BLK), 1)
    rows = jnp.zeros((16, BLK), F32)
    for q in range(4):
        rows = jnp.where(lane == q, got[2 * q, SCAP * PIECE :].astype(F32), rows)
    scales[0] = rows[:SCAP, :4].astype(BF)


def place(got):
    return pl.pallas_call(
        place_body,
        out_shape=[
            jax.ShapeDtypeStruct((1, SCAP, 8 * HALF, BLK), BF),
            jax.ShapeDtypeStruct((1, SCAP, 4), BF),
        ],
        compiler_params=params(),
        cost_estimate=cost(0, 2 * 16 * MSG * BLK * 2),
        name="place_served",
    )(got)


def shards(inputs, cotangent, master, moment, variance, slice_start, block_owner, group_heads):
    me = lax.axis_index(("yh", "yl", "x")).astype(jnp.int32)
    y, x = me // 4, me % 4
    ranks = range(16)

    def along_x(k):
        return [(i, i // 4 * 4 + (i + k) % 4) for i in ranks]

    def along_y(k):
        return [(i, (i + 4 * k) % 16) for i in ranks]

    def send(v, pairs):
        return lax.ppermute(v, ("yh", "yl", "x"), pairs)

    here = jnp.stack([x, y]).astype(jnp.int32)

    def two(k, half):
        return [(k, half), (k, half + 2)]

    def pieces(which, steps, flip=None):
        return mm(here, which, [g0 + g1 for g0, g1 in steps], inputs, cotangent, flip)

    def long_start(which, groups, flip, along):
        fwd, bwd = pieces(which, groups, flip)
        return send(fwd, along(1)), send(bwd, along(-1))

    a_fwd, a_bwd = long_start(
        0, ((two(2, 0), two(2, 1)), (two(1, 1), two(3, 0))), False, along_x
    )
    b_fwd, b_bwd = long_start(
        1, ((two(2, 0), two(3, 0)), (two(1, 1), two(2, 1))), True, along_y
    )
    rest_a = pieces(0, ((two(0, 0), two(0, 1)), (two(1, 0), two(3, 1))))
    rest_b = pieces(1, ((two(0, 0), two(1, 0)), (two(0, 1), two(3, 1))))

    def long_end(rest, out_groups, own_groups, fwd, bwd, along, earlier):
        fwd2, bwd2 = relay(rest, out_groups, fwd, bwd, earlier)
        return long_sum(
            rest, own_groups, send(fwd2, along(1)), send(bwd2, along(-1)), fwd, bwd
        )

    flat = 16 * 18
    ends = jnp.concatenate([slice_start[1:], jnp.full((1,), flat, jnp.int32)])
    is_me = jnp.arange(16, dtype=jnp.int32) == me
    start = jnp.sum(jnp.where(is_me, slice_start, 0))
    end = jnp.sum(jnp.where(is_me, ends, 0))
    odd = x % 2
    info = jnp.stack([start - (18 * me - 9), end - start, odd]).astype(jnp.int32)

    packed = jnp.arange(COLS, dtype=jnp.int32)
    per_group = COLS // GROUPS
    group, within = packed // per_group, packed % per_group
    head_at = group * QPER + jnp.minimum(within, QPER - 1)
    heads = jnp.arange(group_heads.shape[0], dtype=jnp.int32)
    head = jnp.sum(jnp.where(head_at[:, None] == heads, group_heads, 0), axis=1)
    n_heads = group_heads.shape[0]
    column = jnp.where(
        within < QPER, head, jnp.where(within == QPER, n_heads + group, n_heads + GROUPS + group)
    )
    earlier = (block_owner[None, :] == block_owner[:, None]) & (packed[None, :] < packed[:, None])
    spot = block_owner * SCAP + jnp.sum(earlier.astype(jnp.int32), axis=1)
    spots = jnp.arange(8 * SCAP, dtype=jnp.int32)
    table = jnp.sum(jnp.where(spots[:, None] == spot[None, :], column + 1, 0), axis=1) - 1
    pack_info = jnp.concatenate([odd[None], table]).astype(jnp.int32)

    part_a = long_end(rest_a, (2, 3), (0, 1), a_fwd, a_bwd, along_x, (rest_b,))
    part_b = long_end(rest_b, (1, 3), (0, 2), b_fwd, b_bwd, along_y, (rest_a,))

    def short(parts, along):
        return [parts[0]] + [send(parts[k], along(k)) for k in (2, 1, 3)]

    front, back, to_pair, to_cross = slices(
        info, *short(part_a, along_y), *short(part_b, along_x)
    )
    pairs = [(i, i ^ 1) for i in ranks]
    near_by = [(i, i - 1 if i % 2 == 0 else i + 1) for i in ranks if 0 < i < 15]
    far_off = [
        (i, i - 2 if i % 2 == 0 else i + 2)
        for i in ranks
        if 0 <= (i - 2 if i % 2 == 0 else i + 2) < 16
    ]
    inside = send(to_pair, pairs)
    cross = send(to_cross, near_by)

    state = (master, moment, variance)
    keep2, send2 = codes(own_body, 2, 2 * HALF + 16, "codes_of_own", info, front, back, *state)
    got2 = send(send2, pairs)
    keep1, send1, near, far = codes(
        halo_body, 4, HALF + 16, "codes_of_halo", info, inside, cross, *state
    )
    got1 = send(send1, pairs)
    near = send(near, near_by)
    far = send(far, far_off)

    updated = update_state(info, inside, front, back, cross, *state)
    got1, near, far, *updated = lax.optimization_barrier((got1, near, far, *updated))
    out = pack(pack_info, keep2, got2, keep1, got1, near, far)
    got = lax.all_to_all(out, ("z", "core", "yh"), split_axis=0, concat_axis=0, tiled=True)
    got = lax.all_to_all(got, ("yh", "yl", "x"), split_axis=0, concat_axis=0, tiled=True)
    served_blocks, served_scales = place(got)
    return (*updated, served_blocks, served_scales)


def solution(mesh):
    dp, serve = ("yh", "yl", "x"), ("z", "core")
    mesh = Mesh(mesh.devices.reshape(2, 2, 4, 4, 2), dp + serve)
    state = P(serve, dp, None, None)
    return jax.shard_map(
        shards,
        mesh=mesh,
        in_specs=(P(dp, serve), P(dp, None), state, state, state, P(), P(), P()),
        out_specs=(state, state, state, P(serve, None, dp, None), P(serve, None, dp)),
        check_vma=False,
    )
```

```python
import functools

import jax
import jax.numpy as jnp
from jax import lax
from jax.experimental import pallas as pl
from jax.experimental.pallas import tpu as pltpu
from jax.sharding import Mesh
from jax.sharding import PartitionSpec as P

QPER = 16
GROUPS = 2
BLK = 128
HALF = 64
UNIT = 9
WIDE = UNIT * BLK
FIRST = 10 * BLK
LAST = 8 * BLK
TILE = 256
CAP = 36
COLS = 36
SCAP = 9
STEP = 9
PIECE = 32
MSG = SCAP * PIECE + 16

first_bias = 1.0 - 0.9**10
second_bias = 1.0 - 0.95**10

BF = jnp.bfloat16
F32 = jnp.float32


def cost(flops, nbytes):
    return pl.CostEstimate(flops=flops, bytes_accessed=nbytes, transcendentals=0)


def params(mib=20):
    return pltpu.CompilerParams(vmem_limit_bytes=mib * 1024 * 1024)


def mm_products(refs):
    left = jnp.concatenate([ref[...] for ref in refs[:4]], axis=1)
    for n, right in enumerate(refs[4:]):
        prod = lax.dot_general(
            left, right[...], (((0,), (0,)), ((), ())), preferred_element_type=F32
        ).astype(BF)
        for u in range(4):
            yield u, slice(n * TILE, (n + 1) * TILE), prod[u * BLK : (u + 1) * BLK]


def mm_send_body(tiles, spot, *refs):
    fwd, bwd = refs[-2:]
    for u, lanes, prod in mm_products(refs[: 4 + tiles]):
        (fwd if u < 2 else bwd)[u % 2, :, lanes] = prod


def mm_rest_body(spot, *refs):
    for u, lanes, prod in mm_products(refs[:-1]):
        refs[-1][u, :, lanes] = prod


def mm(spot, which, steps, inputs, cotangent, flip=None):
    tok = inputs.shape[0]
    part = FIRST if which == 0 else LAST
    tiles = part // TILE

    def spread(n, g, t):
        (k0, j0), (k1, j1) = steps[0][n], steps[1][n]
        k, j = jnp.where(g == 0, k0, k1), jnp.where(g == 0, j0, j1)
        dx, dy = (k, j) if which == 0 else (j, k)
        return (t[0] + dx) & 3, (t[1] + dy) & 3

    def left(n):
        def at(g, t):
            to_x, to_y = spread(n, g, t)
            return 0, 2 * to_y + (to_x >> 1)

        return pl.BlockSpec((tok, BLK), at)

    def right(n):
        def at(g, t):
            to_x, _ = spread(0, g, t)
            return 0, (to_x & 1) * 9 + (0 if which == 0 else FIRST // TILE) + n

        return pl.BlockSpec((tok, TILE), at)

    if flip is None:
        out_specs = pl.BlockSpec((4, BLK, part), lambda g, t: (g, 0, 0))
        out_shape = jax.ShapeDtypeStruct((8, BLK, part), BF)
    else:
        out_specs = [
            pl.BlockSpec((2, BLK, part), lambda g, t: (g, 0, 0)),
            pl.BlockSpec((2, BLK, part), lambda g, t: ((1 - g) if flip else g, 0, 0)),
        ]
        out_shape = [jax.ShapeDtypeStruct((4, BLK, part), BF)] * 2
    return pl.pallas_call(
        mm_rest_body if flip is None else functools.partial(mm_send_body, tiles),
        grid_spec=pltpu.PrefetchScalarGridSpec(
            num_scalar_prefetch=1,
            grid=(2,),
            in_specs=[left(n) for n in range(4)] + [right(n) for n in range(tiles)],
            out_specs=out_specs,
        ),
        out_shape=out_shape,
        compiler_params=params(56 if flip is None else 60),
        cost_estimate=cost(2 * 2 * 512 * part * tok, 2 * (tok * (part + 512) + 512 * part) * 2),
        name="gradient_pieces" if flip is None else "gradient_to_send",
    )(spot, *([inputs] * 4), *([cotangent] * tiles))


def total(*parts):
    out = parts[0].astype(F32)
    for part in parts[1:]:
        out = out + part.astype(F32)
    return out.astype(BF)


def pair_spec(part, group):
    return pl.BlockSpec((2, BLK, part), lambda s: (group, 0, 0))


def relay_body(to_fwd, to_bwd, fwd, bwd, *refs):
    out_fwd, out_bwd = refs[-2:]
    out_fwd[...] = total(to_fwd[...], fwd[...])
    out_bwd[...] = total(to_bwd[...], bwd[...])


def relay(rest, groups, fwd, bwd, earlier):
    part = rest.shape[2]
    return pl.pallas_call(
        relay_body,
        grid=(1,),
        in_specs=[pair_spec(part, g) for g in (groups[0], groups[1], 0, 0)]
        + [pl.BlockSpec(memory_space=pl.ANY)] * len(earlier),
        out_specs=[pair_spec(part, 0)] * 2,
        out_shape=[jax.ShapeDtypeStruct((2, BLK, part), BF)] * 2,
        compiler_params=params(),
        cost_estimate=cost(4 * BLK * part, 12 * BLK * part * 2),
        name="relay_sums",
    )(rest, rest, fwd, bwd, *earlier)


def long_sum_body(own_even, own_odd, fwd2, bwd2, fwd, bwd, e0, e1, e2, e3):
    for n, (near, far) in enumerate(((e0, e2), (e1, e3))):
        own, second, first = ((own_even, fwd2, bwd), (own_odd, bwd2, fwd))[n]
        near[...] = total(own[0], second[0], first[0])
        far[...] = total(own[1], second[1], first[1])


def long_sum(rest, groups, fwd2, bwd2, fwd, bwd):
    part = rest.shape[2]
    return pl.pallas_call(
        long_sum_body,
        grid=(1,),
        in_specs=[pair_spec(part, g) for g in (groups[0], groups[1], 0, 0, 1, 1)],
        out_specs=[pl.BlockSpec((BLK, part), lambda s: (0, 0))] * 4,
        out_shape=[jax.ShapeDtypeStruct((BLK, part), BF)] * 4,
        compiler_params=params(52),
        cost_estimate=cost(8 * BLK * part, 16 * BLK * part * 2),
        name="long_sums",
    )(rest, rest, fwd2, bwd2, fwd, bwd)


def slice_body(info, *refs):
    front, back, to_pair, to_cross = refs[8:]
    first = total(*(ref[...] for ref in refs[:4]))
    last = total(*(ref[...] for ref in refs[4:8]))
    front[...] = first[:, :WIDE]
    back[:, :BLK] = first[:, WIDE:]
    back[:, BLK:] = last

    @pl.when(info[2] == 0)
    def _():
        to_pair[...] = back[...]
        to_cross[...] = front[...]

    @pl.when(info[2] == 1)
    def _():
        to_pair[...] = front[...]
        to_cross[...] = back[...]


def slices(info, *parts):
    return pl.pallas_call(
        slice_body,
        grid_spec=pltpu.PrefetchScalarGridSpec(
            num_scalar_prefetch=1,
            grid=(1,),
            in_specs=[pl.BlockSpec(v.shape, lambda s, t: (0, 0)) for v in parts],
            out_specs=[pl.BlockSpec((BLK, WIDE), lambda s, t: (0, 0))] * 4,
        ),
        out_shape=[jax.ShapeDtypeStruct((BLK, WIDE), BF)] * 4,
        compiler_params=params(),
        cost_estimate=cost(8 * BLK * WIDE, 12 * BLK * WIDE * 2),
        name="slices",
    )(info, *parts)


def adam_step(old, moment, variance, grad):
    mom = 0.9 * moment + 0.1 * grad
    var = 0.95 * variance + 0.05 * (grad * grad)
    new = old - 0.02 * (
        (mom * (1.0 / first_bias)) / (jnp.sqrt(var * (1.0 / second_bias)) + 1e-08) + 0.1 * old
    )
    return new, mom, var


def unit_of(place):
    unit = lax.div(place, UNIT)
    return unit, pl.ds(pl.multiple_of((place - unit * UNIT) * BLK, BLK), BLK)


def wrap(slot):
    slot = jnp.where(slot < 0, slot + CAP, slot)
    return jnp.where(slot >= CAP, slot - CAP, slot)


def code_body(units, info, first, second, master, moment, variance, mine, other, scales):
    off, length, odd = info[0], info[1], info[2]
    for n, (unit, grads) in enumerate(zip(units, (first, second))):
        for b in range(UNIT):
            slot = wrap(unit * UNIT + b - off)
            live = slot < length
            lanes = slice(b * BLK, (b + 1) * BLK)
            grad = grads[:, lanes].astype(F32)
            new, _, _ = adam_step(master[0, slot], moment[0, slot], variance[0, slot], grad)
            peak = jnp.max(jnp.abs(new), axis=(0, 1), keepdims=True)
            scale = (peak + 1e-06).astype(BF).astype(F32)
            code = jnp.where(live, new * (1.0 / scale), 0.0).astype(BF)
            top, low = code[:HALF], code[HALF:]
            mine[n, :, lanes] = jnp.where(odd == 1, low, top)
            other[n, :, lanes] = jnp.where(odd == 1, top, low)
            scales[n, :, lanes] = jnp.broadcast_to(jnp.where(live, scale, 0.0), (8, BLK))


def scale_rows(scales, rows):
    return jnp.concatenate(
        [scales[n, 0:1] for n in rows] + [jnp.zeros((16 - len(rows), WIDE), F32)], axis=0
    ).astype(BF)


def own_body(info, a, b, master, moment, variance, keep, send, mine, other, scales):
    code_body((1, 2), info, a, b, master, moment, variance, mine, other, scales)
    tail = scale_rows(scales, (0, 1))
    for ref, held in ((keep, mine), (send, other)):
        ref[:HALF] = held[0]
        ref[HALF : 2 * HALF] = held[1]
        ref[2 * HALF :] = tail


def halo_body(
    info, inside, cross, master, moment, variance, keep, send, near, far, mine, other, scales
):
    odd = info[2]
    units = (3 - 3 * odd, 3 * odd)
    code_body(units, info, inside, cross, master, moment, variance, mine, other, scales)
    for n, outs in enumerate(((keep, send), (far, near))):
        tail = scale_rows(scales, (n,))
        for ref, held in zip(outs, (mine, other)):
            ref[:HALF] = held[n]
            ref[HALF:] = tail


def codes(body, n_out, rows, name, info, a, b, master, moment, variance):
    whole = lambda v: pl.BlockSpec(v.shape, lambda s, t: (0,) * v.ndim)
    return pl.pallas_call(
        body,
        grid_spec=pltpu.PrefetchScalarGridSpec(
            num_scalar_prefetch=1,
            grid=(1,),
            in_specs=[whole(v) for v in (a, b, master, moment, variance)],
            out_specs=[pl.BlockSpec((rows, WIDE), lambda s, t: (0, 0))] * n_out,
            scratch_shapes=[
                pltpu.VMEM((2, HALF, WIDE), BF),
                pltpu.VMEM((2, HALF, WIDE), BF),
                pltpu.VMEM((2, 8, WIDE), F32),
            ],
        ),
        out_shape=[jax.ShapeDtypeStruct((rows, WIDE), BF)] * n_out,
        compiler_params=params(),
        cost_estimate=cost(18 * 16384 * 30, 36 * 16384 * 12),
        name=name,
    )(info, a, b, master, moment, variance)


def state_body(
    info, inside, front, back, cross, master, moment, variance,
    new_master, new_moment, new_variance, window,
):
    step = pl.program_id(0)
    off, length = info[0], info[1]

    @pl.when(step == 0)
    def _():
        window[1] = front[...]
        window[2] = back[...]
        window[3 - 3 * info[2]] = inside[...]
        window[3 * info[2]] = cross[...]

    for n in range(STEP):
        slot = step * STEP + n
        unit, lanes = unit_of(wrap(off + slot))
        grad = jnp.where(slot < length, window[unit, :, lanes].astype(F32), 0.0)
        new_master[0, n], new_moment[0, n], new_variance[0, n] = adam_step(
            master[0, n], moment[0, n], variance[0, n], grad
        )


def update_state(info, inside, front, back, cross, master, moment, variance):
    state = pl.BlockSpec((1, STEP, BLK, BLK), lambda s, t: (0, s, 0, 0))
    return pl.pallas_call(
        state_body,
        grid_spec=pltpu.PrefetchScalarGridSpec(
            num_scalar_prefetch=1,
            grid=(CAP // STEP,),
            in_specs=[pl.BlockSpec((BLK, WIDE), lambda s, t: (0, 0))] * 4 + [state] * 3,
            out_specs=[state] * 3,
            scratch_shapes=[pltpu.VMEM((4, BLK, WIDE), BF)],
        ),
        out_shape=[jax.ShapeDtypeStruct(master.shape, F32)] * 3,
        compiler_params=params(32),
        cost_estimate=cost(36 * 16384 * 20, 36 * 16384 * 26),
        name="update_state",
    )(info, inside, front, back, cross, master, moment, variance)


def pack_body(info, keep2, got2, keep1, got1, near, far, out, row, tails):
    def half(ref, n):
        return ref[n * HALF : (n + 1) * HALF]

    def tail(ref, n):
        at = ref.shape[0] - 16
        return ref[at:].astype(F32)[n : n + 1]

    own, pair = [(keep2, 0), (keep2, 1)], [(got2, 0), (got2, 1)]
    inner_own, inner_pair, by, on = (keep1, 0), (got1, 0), (near, 0), (far, 0)

    def fill(units):
        for q, parts in enumerate(units):
            (a, m), (b, n) = parts
            row[q] = half(a, m) + half(b, n)
            tails[q, 0:1] = tail(a, m) + tail(b, n)

    @pl.when(info[0] == 0)
    def _():
        fill(((own[0], by), (own[1], inner_pair), (pair[0], inner_own), (pair[1], on)))

    @pl.when(info[0] == 1)
    def _():
        fill(((pair[0], on), (pair[1], inner_own), (own[0], inner_pair), (own[1], by)))

    def owner(o, carry):
        rows = []
        for t in range(SCAP):
            col = info[1 + o * SCAP + t]
            unit, lanes = unit_of(jnp.maximum(col, 0))
            piece = row[unit, :, lanes]
            piece = jnp.where(col >= 0, piece, jnp.zeros_like(piece))
            for part in range(2):
                out[2 * o + part, t * PIECE : (t + 1) * PIECE] = piece[
                    part * PIECE : (part + 1) * PIECE
                ]
            rows.append(jnp.where(col >= 0, tails[unit, :, lanes][0:1], 0.0))
        rows.append(jnp.zeros((16 - SCAP, BLK), F32))
        last = jnp.concatenate(rows, axis=0).astype(BF)
        for part in range(2):
            out[2 * o + part, SCAP * PIECE :] = last
        return carry

    lax.fori_loop(0, 8, owner, 0)


def pack(info, *parts):
    return pl.pallas_call(
        pack_body,
        grid_spec=pltpu.PrefetchScalarGridSpec(
            num_scalar_prefetch=1,
            grid=(1,),
            in_specs=[pl.BlockSpec(a.shape, lambda s, t: (0, 0)) for a in parts],
            out_specs=pl.BlockSpec((16, MSG, BLK), lambda s, t: (0, 0, 0)),
            scratch_shapes=[pltpu.VMEM((4, HALF, WIDE), BF), pltpu.VMEM((4, 8, WIDE), F32)],
        ),
        out_shape=jax.ShapeDtypeStruct((16, MSG, BLK), BF),
        compiler_params=params(),
        cost_estimate=cost(0, 3 * 16 * MSG * BLK * 2),
        name="pack_by_owner",
    )(info, *parts)


def place_body(got, out, scales):
    for src in range(16):
        upper, low, x = src // 8, src // 4 % 2, src % 4
        at = (2 * low + x // 2) * BLK + (x % 2) * HALF + upper * PIECE
        for t in range(SCAP):
            out[0, t, at : at + PIECE] = got[src, t * PIECE : (t + 1) * PIECE]
    lane = lax.broadcasted_iota(jnp.int32, (16, BLK), 1)
    rows = jnp.zeros((16, BLK), F32)
    for q in range(4):
        rows = jnp.where(lane == q, got[2 * q, SCAP * PIECE :].astype(F32), rows)
    scales[0] = rows[:SCAP, :4].astype(BF)


def place(got):
    return pl.pallas_call(
        place_body,
        out_shape=[
            jax.ShapeDtypeStruct((1, SCAP, 8 * HALF, BLK), BF),
            jax.ShapeDtypeStruct((1, SCAP, 4), BF),
        ],
        compiler_params=params(),
        cost_estimate=cost(0, 2 * 16 * MSG * BLK * 2),
        name="place_served",
    )(got)


def shards(inputs, cotangent, master, moment, variance, slice_start, block_owner, group_heads):
    me = lax.axis_index(("yh", "yl", "x")).astype(jnp.int32)
    y, x = me // 4, me % 4
    ranks = range(16)

    def along_x(k):
        return [(i, i // 4 * 4 + (i + k) % 4) for i in ranks]

    def along_y(k):
        return [(i, (i + 4 * k) % 16) for i in ranks]

    def send(v, pairs):
        return lax.ppermute(v, ("yh", "yl", "x"), pairs)

    here = jnp.stack([x, y]).astype(jnp.int32)

    def two(k, half):
        return [(k, half), (k, half + 2)]

    def pieces(which, steps, flip=None):
        return mm(here, which, [g0 + g1 for g0, g1 in steps], inputs, cotangent, flip)

    def long_start(which, groups, flip, along):
        fwd, bwd = pieces(which, groups, flip)
        return send(fwd, along(1)), send(bwd, along(-1))

    a_fwd, a_bwd = long_start(
        0, ((two(2, 0), two(2, 1)), (two(1, 1), two(3, 0))), False, along_x
    )
    b_fwd, b_bwd = long_start(
        1, ((two(2, 0), two(3, 0)), (two(1, 1), two(2, 1))), True, along_y
    )
    rest_a = pieces(0, ((two(0, 0), two(0, 1)), (two(1, 0), two(3, 1))))
    rest_b = pieces(1, ((two(0, 0), two(1, 0)), (two(0, 1), two(3, 1))))

    def long_end(rest, out_groups, own_groups, fwd, bwd, along, earlier):
        fwd2, bwd2 = relay(rest, out_groups, fwd, bwd, earlier)
        return long_sum(
            rest, own_groups, send(fwd2, along(1)), send(bwd2, along(-1)), fwd, bwd
        )

    flat = 16 * 18
    ends = jnp.concatenate([slice_start[1:], jnp.full((1,), flat, jnp.int32)])
    is_me = jnp.arange(16, dtype=jnp.int32) == me
    start = jnp.sum(jnp.where(is_me, slice_start, 0))
    end = jnp.sum(jnp.where(is_me, ends, 0))
    odd = x % 2
    info = jnp.stack([start - (18 * me - 9), end - start, odd]).astype(jnp.int32)

    packed = jnp.arange(COLS, dtype=jnp.int32)
    per_group = COLS // GROUPS
    group, within = packed // per_group, packed % per_group
    head_at = group * QPER + jnp.minimum(within, QPER - 1)
    heads = jnp.arange(group_heads.shape[0], dtype=jnp.int32)
    head = jnp.sum(jnp.where(head_at[:, None] == heads, group_heads, 0), axis=1)
    n_heads = group_heads.shape[0]
    column = jnp.where(
        within < QPER, head, jnp.where(within == QPER, n_heads + group, n_heads + GROUPS + group)
    )
    earlier = (block_owner[None, :] == block_owner[:, None]) & (packed[None, :] < packed[:, None])
    spot = block_owner * SCAP + jnp.sum(earlier.astype(jnp.int32), axis=1)
    spots = jnp.arange(8 * SCAP, dtype=jnp.int32)
    table = jnp.sum(jnp.where(spots[:, None] == spot[None, :], column + 1, 0), axis=1) - 1
    pack_info = jnp.concatenate([odd[None], table]).astype(jnp.int32)

    part_a = long_end(rest_a, (2, 3), (0, 1), a_fwd, a_bwd, along_x, (rest_b,))
    part_b = long_end(rest_b, (1, 3), (0, 2), b_fwd, b_bwd, along_y, (rest_a,))

    def short(parts, along):
        return [parts[0]] + [send(parts[k], along(k)) for k in (2, 1, 3)]

    front, back, to_pair, to_cross = slices(
        info, *short(part_a, along_y), *short(part_b, along_x)
    )
    pairs = [(i, i ^ 1) for i in ranks]
    near_by = [(i, i - 1 if i % 2 == 0 else i + 1) for i in ranks if 0 < i < 15]
    far_off = [
        (i, i - 2 if i % 2 == 0 else i + 2)
        for i in ranks
        if 0 <= (i - 2 if i % 2 == 0 else i + 2) < 16
    ]
    inside = send(to_pair, pairs)
    cross = send(to_cross, near_by)

    state = (master, moment, variance)
    keep2, send2 = codes(own_body, 2, 2 * HALF + 16, "codes_of_own", info, front, back, *state)
    got2 = send(send2, pairs)
    keep1, send1, near, far = codes(
        halo_body, 4, HALF + 16, "codes_of_halo", info, inside, cross, *state
    )
    got1 = send(send1, pairs)
    near = send(near, near_by)
    far = send(far, far_off)

    updated = update_state(info, inside, front, back, cross, *state)
    got1, near, far, *updated = lax.optimization_barrier((got1, near, far, *updated))
    out = pack(pack_info, keep2, got2, keep1, got1, near, far)
    got = lax.all_to_all(out, ("z", "core", "yh"), split_axis=0, concat_axis=0, tiled=True)
    got = lax.all_to_all(got, ("yh", "yl", "x"), split_axis=0, concat_axis=0, tiled=True)
    served_blocks, served_scales = place(got)
    return (*updated, served_blocks, served_scales)


def solution(mesh):
    dp, serve = ("yh", "yl", "x"), ("z", "core")
    mesh = Mesh(mesh.devices.reshape(2, 2, 4, 4, 2), dp + serve)
    state = P(serve, dp, None, None)
    return jax.shard_map(
        shards,
        mesh=mesh,
        in_specs=(P(dp, serve), P(dp, None), state, state, state, P(), P(), P()),
        out_specs=(state, state, state, P(serve, None, dp, None), P(serve, None, dp)),
        check_vma=False,
    )
```
